256 devices in a mesh: tile: 64 (over x, y, z_hi), lev: 4 (over z_lo, core).
Axes of the slice: x: 4, y: 4, z: 8 (z_hi: 4, z_lo: 2; z = z_hi * 2 + z_lo), core: 2. Of those that a mesh axis runs over, the one named last changes fastest.
Arguments:
- state: float32 [4, 32, 256, 128], P(None, 'lev', 'tile'), may hold values from -6 to 6
- coef_x: float32 [32, 256, 128], P('lev', 'tile'), may hold values from 0.2 to 0.6
- coef_y: float32 [32, 256, 128], P('lev', 'tile'), may hold values from 0.2 to 0.6
- coef_z: float32 [32, 256, 128], P('lev', 'tile'), may hold values from 0.2 to 0.6
- slope: float32 [32, 256, 128], P('lev', 'tile'), may hold values from -0.3 to 0.3
- compress: float32 [32, 256, 128], P('lev', 'tile'), may hold values from 0.2 to 0.6
- ground: int32 [256, 128], P('tile'), may hold values from 0 to 8
- w_in: bfloat16 [4, 512], replicated, may hold values from -3 to 3
- level_table: float32 [32, 512], replicated, may hold values from -6 to 6
- gain_attn: float32 [512], replicated, may hold values from 0.1 to 1.9
- w_query: bfloat16 [512, 512], replicated, may hold values from -0.25 to 0.25
- w_key: bfloat16 [512, 512], replicated, may hold values from -0.25 to 0.25
- w_value: bfloat16 [512, 512], replicated, may hold values from -0.25 to 0.25
- w_mix: bfloat16 [512, 512], replicated, may hold values from -0.25 to 0.25
- temper: float32 [8], replicated, may hold values from 0.5 to 64, as said below
- gain_head: float32 [512], replicated, may hold values from 0.1 to 1.9
- w_tend: bfloat16 [512, 4], replicated, may hold values from -0.25 to 0.25
Outputs:
- updated: float32 [4, 32, 256, 128], P(None, 'lev', 'tile')
The draws below stay inside these ranges and needn't reach their ends.
Inputs may be any that keep to these rules, and one draw needn't show every extreme that they name: `temper`: positive score scales of the heads.
All inputs are finite; a program needn't handle non-finite values.
Results may differ from the reference program's by a relative error of at most 0.024.
Values may be sent and summed in bfloat16 or wider, within the bound.
A program may use at most 128 MiB of HBM per device.

```python
import math
import jax
import jax.numpy as jnp
from jax import lax

D = 512
H = 8
L = 32
BY = 128
NX = 256
SUBSTEPS = 3


def draw_temper(key, part):
    key = jax.random.fold_in(key, 5)
    spread = jax.random.uniform(key, (H,), jnp.float32)
    lower, upper = (0.5, 4.0)
    return jnp.exp(jnp.log(lower) + spread * (jnp.log(upper) - jnp.log(lower))).astype(jnp.float32)


def place_ends(values, rng, least, high):
    extent = values.shape
    place = [jax.random.randint(jax.random.fold_in(rng, axis), (), 0, extent[axis]) for axis in range(len(extent))]
    values = values.at[tuple(place)].set(least)
    longest = extent.index(max(extent))
    place[longest] = (place[longest] + 1) % extent[longest]
    return values.at[tuple(place)].set(high)


def shard_levels(stream_key, dims, shards, low, largest):
    loudness, own = 1.0, jax.random.fold_in(stream_key, 6)
    for axis_at, blocks in shards:
        draws = jnp.exp(jax.random.uniform(jax.random.fold_in(own, axis_at), (blocks,), jnp.float32, low / len(shards), largest / len(shards)))
        loudness = loudness * jnp.repeat(draws, dims[axis_at] // blocks).reshape([-1 if axis == axis_at else 1 for axis in range(len(dims))])
    return loudness


def gaussian(stream_key, dims, deviation, bound, pieces=(), kind=jnp.bfloat16):
    array = deviation * jax.random.normal(stream_key, dims, jnp.float32)
    if pieces:
        array = array * shard_levels(stream_key, dims, pieces, -0.22, 0.18)
    return jnp.clip(array, -bound, bound).astype(kind)


def setup_inputs(seed: int = 0) -> dict:
    key_of = jax.random.split(jax.random.key(seed), 18)
    return {
        "state": gaussian(key_of[0], (4, L, NX, BY), 1.0, 6.0, ((1, 4), (2, 64)), jnp.float32),
        "coef_x": jnp.clip(0.2 + 0.400000021 * jax.random.uniform(key_of[1], (L, NX, BY), jnp.float32) ** shard_levels(key_of[1], (L, NX, BY), ((0, 4), (1, 64)), -0.2, 0.2), 0.2, 0.6),
        "coef_y": jnp.clip(0.2 + 0.400000021 * jax.random.uniform(key_of[2], (L, NX, BY), jnp.float32) ** shard_levels(key_of[2], (L, NX, BY), ((0, 4), (1, 64)), -0.2, 0.2), 0.2, 0.6),
        "coef_z": jnp.clip(0.2 + 0.400000021 * jax.random.uniform(key_of[3], (L, NX, BY), jnp.float32) ** shard_levels(key_of[3], (L, NX, BY), ((0, 4), (1, 64)), -0.2, 0.2), 0.2, 0.6),
        "slope": jnp.clip(jax.random.uniform(key_of[4], (L, NX, BY), jnp.float32, -0.3, 0.3) * shard_levels(key_of[4], (L, NX, BY), ((0, 4), (1, 64)), -0.4, 0.0), -0.3, 0.3),
        "compress": jnp.clip(0.2 + 0.400000021 * jax.random.uniform(key_of[5], (L, NX, BY), jnp.float32) ** shard_levels(key_of[5], (L, NX, BY), ((0, 4), (1, 64)), -0.2, 0.2), 0.2, 0.6),
        "ground": place_ends(jax.random.randint(key_of[6], (NX, BY), 0, L // 4 + 1), jax.random.fold_in(key_of[6], 1), 0, (L // 4 + 1) - 1).astype(jnp.int32),
        "w_in": gaussian(key_of[7], (4, D), 4 ** -0.5, 3.0),
        "level_table": gaussian(key_of[8], (L, D), 1.0, 6.0, (), jnp.float32),
        "gain_attn": jnp.clip(1.0 + 0.18 * jax.random.normal(key_of[9], (D,), jnp.float32), 0.1, 1.9),
        "w_query": gaussian(key_of[10], (D, D), D ** -0.5, 0.25),
        "w_key": gaussian(key_of[11], (D, D), D ** -0.5, 0.25),
        "w_value": gaussian(key_of[12], (D, D), D ** -0.5, 0.25),
        "w_mix": gaussian(key_of[13], (D, D), D ** -0.5, 0.25),
        "temper": draw_temper(jax.random.fold_in(key_of[17], 71), 0),
        "gain_head": jnp.clip(1.0 + 0.18 * jax.random.normal(key_of[15], (D,), jnp.float32), 0.1, 1.9),
        "w_tend": gaussian(key_of[16], (D, 4), D ** -0.5, 0.25),
    }


EPS = 1e-06

def acoustic(padded, metrics, coef_y, compress):
    pressure = padded[0]
    east_wind = padded[1]
    north_wind = padded[2]
    upward = padded[3]
    grad_x = metrics[0]
    slope_pad = metrics[1]
    grad_z = metrics[2]
    inner_k = pressure[1:-1]
    east_new = east_wind[1:-1, :-1] - grad_x[1:-1, :-1] * (inner_k[:, 1:] - inner_k[:, :-1]) - 0.5 * slope_pad[1:-1, :-1] * (pressure[2:, :-1] - pressure[:-2, :-1])
    inner_x = pressure[:, 1:-1]
    upward_new = upward[:-1, 1:-1] - grad_z[:-1, 1:-1] * (inner_x[1:] - inner_x[:-1])
    centre = pressure[1:-1, 1:-1]
    north_new = north_wind[1:-1, 1:-1] - coef_y * (jnp.roll(centre, -1, axis=2) - centre)
    divergence = east_new[:, 1:] - east_new[:, :-1] + (north_new - jnp.roll(north_new, 1, axis=2)) + (upward_new[1:] - upward_new[:-1])
    pressure_new = centre - compress * divergence
    return jnp.stack([pressure_new, east_new[:, 1:], north_new, upward_new[1:]])

def multiply(pattern, first_op, second_op):
    return jnp.einsum(pattern, first_op.astype(jnp.float32), second_op.astype(jnp.float32))

def rms_scale(values, over_dim):
    return values * lax.rsqrt(lax.optimization_barrier(jnp.mean(values * values, axis=over_dim, keepdims=True)) + EPS)

def physics(embedded, ground_cols, gain_attn, w_query, w_key, w_value, w_mix, temper, gain_head, w_tend):
    model_width, levels, columns = embedded.shape
    head_count = temper.shape[0]
    head_size = model_width // head_count
    stream = embedded.astype(jnp.float32)
    normed = (rms_scale(stream, 0) * gain_attn[:, None, None]).astype(jnp.bfloat16)

    def heads_of(weight):
        return multiply('dlc,de->elc', normed, weight).reshape(head_count, head_size, levels, columns)
    query_heads = rms_scale(heads_of(w_query), 1).astype(jnp.bfloat16)
    key_heads = rms_scale(heads_of(w_key), 1).astype(jnp.bfloat16)
    value_heads = heads_of(w_value).astype(jnp.bfloat16)
    scores = multiply('hjlc,hjmc->hlmc', query_heads, key_heads) * (temper / math.sqrt(head_size))[:, None, None, None]
    over_ground = jnp.arange(levels, dtype=jnp.int32)[:, None] >= ground_cols[None, :]
    scores = jnp.where(over_ground[None, None], scores, -1e+30)
    peak = lax.optimization_barrier(jnp.max(scores, axis=2, keepdims=True))
    weights = jnp.exp(scores - peak)
    probabilities = (weights / lax.optimization_barrier(jnp.sum(weights, axis=2, keepdims=True))).astype(jnp.bfloat16)
    mixed_heads = multiply('hlmc,hjmc->hjlc', probabilities, value_heads).astype(jnp.bfloat16)
    mixed_heads = mixed_heads.reshape(model_width, levels, columns)
    stream = stream + multiply('dlc,de->elc', mixed_heads, w_mix)
    final_normed = (rms_scale(stream, 0) * gain_head[:, None, None]).astype(jnp.bfloat16)
    return multiply('dlc,df->flc', final_normed, w_tend)

def reference(state, coef_x, coef_y, coef_z, slope, compress, ground, w_in, level_table, gain_attn, w_query, w_key, w_value, w_mix, temper, gain_head, w_tend):
    pad_spec = ((0, 0), (1, 1), (1, 1), (0, 0))
    metrics = jnp.pad(jnp.stack([coef_x, slope, coef_z]), pad_spec)
    current = state
    for substep in range(SUBSTEPS):
        current = acoustic(jnp.pad(current, pad_spec), metrics, coef_y, compress)
    features = current.astype(jnp.bfloat16)

    def one_row(packed):
        row_fields, row_ground = packed
        embedded = (multiply('flc,fd->dlc', row_fields, w_in) + jnp.transpose(level_table)[:, :, None]).astype(jnp.bfloat16)
        return physics(embedded, row_ground, gain_attn, w_query, w_key, w_value, w_mix, temper, gain_head, w_tend)
    tendency = lax.map(one_row, (jnp.moveaxis(features, 2, 0), ground))
    return current + jnp.moveaxis(tendency, 0, 2)
```

```python
import math

import jax
import jax.numpy as jnp
from jax import lax
from jax.experimental import pallas as pl
from jax.experimental.pallas import tpu as pltpu
from jax.sharding import PartitionSpec as P

EPS = 1e-6
F32, BF16 = jnp.float32, jnp.bfloat16
LOG2E = math.log2(math.e)
HEADS, WIDTH, LEVELS, CELLS = 8, 512, 32, 128
HS = WIDTH // HEADS
X = 40


def dot(a, b):
    return jnp.dot(a, b, preferred_element_type=F32)


def dot_t(a, b):
    return lax.dot_general(a, b, (((1,), (1,)), ((), ())), precision=lax.Precision.HIGHEST, preferred_element_type=F32)


def split3(a):
    hi = a.astype(BF16).astype(F32)
    mid = (a - hi).astype(BF16).astype(F32)
    return hi, mid, a - hi - mid


def spread(a):
    hi, mid, lo = split3(a)
    return (hi + pltpu.roll(mid, X, 1) + pltpu.roll(lo, 2 * X, 1)).astype(BF16)


def prepare_maps(w_in, table, gain_attn, wq, wk, wv, wm, gain_head, w_tend, temper, lk, ls, lf, tcol):
    emb = jnp.concatenate([w_in[...].astype(F32), jnp.zeros((4, WIDTH), F32), table[...]], axis=0)
    xg3 = jnp.concatenate(split3(emb * gain_attn[...]), axis=0).astype(BF16)

    def through(w):
        a = dot(xg3, w[...])
        return a[:X] + a[X : 2 * X] + a[2 * X :]

    aq, ak, av = through(wq), through(wk), through(wv)
    pad = jnp.zeros((128 - X, WIDTH), F32)
    aq_p = jnp.concatenate([aq, pad], axis=0)
    ak_p = jnp.concatenate([ak, pad], axis=0)
    head = lax.broadcasted_iota(jnp.int32, (X, WIDTH), 1) // HS

    def by_head(a):
        return jnp.concatenate([jnp.where(head == h, a, 0.0) for h in range(HEADS)], axis=0)

    kb = by_head(ak)
    qb = by_head(aq)
    s_map = dot_t(kb, aq_p)
    kk = dot_t(kb, ak_p)
    qq = dot_t(qb, aq_p)
    ee = dot_t(emb, jnp.concatenate([emb, pad], axis=0))
    lane = lax.broadcasted_iota(jnp.int32, (1, 128), 1)
    twice = jnp.where(lane < 8, 1.0, 2.0)
    r40 = lax.broadcasted_iota(jnp.int32, (X, 128), 0)
    l40 = lax.broadcasted_iota(jnp.int32, (X, 128), 1)
    diag = (r40 == l40) & (r40 >= 8)

    def norm_rows(g):
        return [g[i : i + 1] * twice for i in range(4)] + [jnp.sum(jnp.where(diag, g, 0.0), axis=0, keepdims=True)]

    def norm_map(gram):
        per = [norm_rows(gram[X * h : X * h + X]) for h in range(HEADS)]
        return jnp.concatenate([per[h][i] for i in range(5) for h in range(HEADS)], axis=0)

    e_rows = norm_rows(ee) + [jnp.zeros((3, 128), F32)]
    lk[...] = spread(jnp.concatenate([norm_map(kk)] + e_rows, axis=0))
    ls[0:320] = spread(s_map)
    ls[320:360] = spread(norm_map(qq))
    ls[360:368] = jnp.zeros((8, 128), BF16)

    vh, vm, _ = split3(by_head(av))
    c = dot(vh.astype(BF16), wm[...]) + dot(vm.astype(BF16), wm[...])
    eh, em, el = split3(emb)
    rows = [c[X * h + 8 : X * h + X] for h in range(HEADS)]
    rows += [jnp.broadcast_to(c[X * h + i : X * h + i + 1], (8, WIDTH)) for h in range(HEADS) for i in range(4)]
    rows += [eh, em, el, jnp.zeros((8, WIDTH), F32)]
    lft = jnp.concatenate(rows, axis=0)
    wt = jnp.concatenate([w_tend[...].astype(F32), jnp.zeros((12, WIDTH), F32)], axis=0) * gain_head[...]
    t = dot_t(wt, lft)
    th = t[:8].astype(BF16).astype(F32)
    lf[0:512] = lft.T.astype(BF16)
    lf[512:528] = jnp.concatenate([th, t[:8] - th], axis=0).astype(BF16)
    row8 = lax.broadcasted_iota(jnp.int32, (8, 128), 0)
    tc = jnp.zeros((8, 128), F32)
    for h in range(HEADS):
        tc = jnp.where(row8 == h, temper[h] * (LOG2E / math.sqrt(HS)), tc)
    tcol[...] = tc


def token_rows(fl, l):
    lev = lax.broadcasted_iota(jnp.int32, (LEVELS, CELLS), 0) == l
    one = jnp.concatenate([fl[l], lev.astype(F32)], axis=0)
    return jnp.concatenate([one, one, one, jnp.zeros((8, CELLS), F32)], axis=0).astype(BF16)


def norms_at(out, f, base, epsq, scale):
    n = out[base + 32 : base + 40]
    for i in range(4):
        n = n + f[i : i + 1] * out[base + 8 * i : base + 8 * i + 8]
    return lax.rsqrt(jnp.maximum(n, 0.0) * (1.0 / HS) + epsq) * scale


def key_pass(l, fl, lk, rk, rs, eq):
    out = dot(lk[...], token_rows(fl, l))
    f = fl[l]
    n = out[44:45]
    for i in range(4):
        n = n + f[i : i + 1] * out[40 + i : 41 + i]
    ms = jnp.maximum(n, 0.0) * (1.0 / WIDTH) + EPS
    rs[pl.ds(l, 1), :] = lax.rsqrt(ms)
    eq[pl.ds(l, 1), :] = EPS * ms
    rk[:, l, :] = norms_at(out, f, 0, EPS * ms, 1.0)


def query_pass(l0, fl, fm, bias, ls, lf, tcol, rk, rs, eq, ot):
    x = jnp.concatenate([token_rows(fl, l0), token_rows(fl, l0 + 1)], axis=1)
    out = dot(ls[...], x)
    parts = []
    for a in range(2):
        o = out[:, 128 * a : 128 * a + 128]
        rq = norms_at(o, fl[l0 + a], 320, eq[pl.ds(l0 + a, 1), :], tcol[...])
        probs, sums = [], []
        for h in range(HEADS):
            s = o[X * h + 8 : X * h + X]
            for i in range(4):
                s = s + fm[i] * o[X * h + i : X * h + i + 1]
            s = s * rk[h] * rq[h : h + 1] + bias[...]
            p = jnp.exp2(s - jnp.max(s, axis=0, keepdims=True))
            p = p * (1.0 / jnp.sum(p, axis=0, keepdims=True)) * rs[...]
            probs.append(p)
            for i in range(4):
                z = p * fm[i]
                sums.append(z[0:8] + z[8:16] + z[16:24] + z[24:32])
        parts.append(jnp.concatenate(probs + sums, axis=0).astype(BF16))
    rhs = jnp.concatenate([jnp.concatenate(parts, axis=1), x], axis=0)
    fin = dot(lf[...], rhs)
    stream = fin[:512]
    ms = jnp.mean(stream * stream, axis=0, keepdims=True)
    tend = (fin[512:520] + fin[520:528]) * lax.rsqrt(ms + EPS)
    ot[l0] = tend[:, :128]
    ot[l0 + 1] = tend[:, 128:]


ROWS = 4
KL = 8
MESH = pl.DeviceIdType.MESH


def level_above(a, row):
    k = lax.broadcasted_iota(jnp.int32, (KL, CELLS), 0)
    return jnp.where(k == KL - 1, row, pltpu.roll(a, KL - 1, 0))


def level_below(a, row):
    k = lax.broadcasted_iota(jnp.int32, (KL, CELLS), 0)
    return jnp.where(k == 0, row, pltpu.roll(a, 1, 0))


def substep(p, p_lo, p_hi, u, v, w, w_lo, cx, sl, cy, cz, cz_lo, cp):
    up = [level_above(p[i], p_hi[i]) for i in range(ROWS + 1)]
    down = [level_below(p[i], p_lo[i]) for i in range(ROWS + 1)]
    u = [u[i] - cx[i] * (p[i + 1] - p[i]) - 0.5 * sl[i] * (up[i] - down[i]) for i in range(ROWS + 1)]
    new_p, new_v, new_w, new_w_lo = [], [], [], []
    for x in range(ROWS):
        c = p[x + 1]
        wx = w[x] - cz[x] * (up[x + 1] - c)
        wl = w_lo[x] - cz_lo[x] * (c[0:1] - p_lo[x + 1])
        vx = v[x] - cy[x] * (pltpu.roll(c, CELLS - 1, 1) - c)
        div = (u[x + 1] - u[x]) + (vx - pltpu.roll(vx, 1, 1)) + (wx - level_below(wx, wl))
        new_p.append(c - cp[x] * div)
        new_v.append(vx)
        new_w.append(wx)
        new_w_lo.append(wl)
    return new_p, u, new_v, new_w, new_w_lo


def whole(tiles, levs, state, coef_x, coef_y, coef_z, slope, compress, ground, temper,
          w_in, table, gain_attn, gain_head, w_tend, wq_hbm, wk_hbm, wv_hbm, wm_hbm, out,
          fl, ot, lk, ls, lf, tcol, rk, rs, eq, bias, fm,
          wq, wk, wv, wm, w_sem,
          up0_s, up0_r, up_s, up_r, dn_s, dn_r, kup0_s, kup0_r, kup_s, kup_r, kdn_s, kdn_r,
          cu_s, cu_r, cd_s, cd_r, halo_ss, halo_rs,
          feat_s, feat_r, feat_ss, feat_rs, tend_s, tend_r, tend_ss, tend_rs, cur):
    tile, lev = lax.axis_index("tile"), lax.axis_index("lev")
    east, west = lax.rem(tile + 1, tiles), lax.rem(tile + tiles - 1, tiles)
    above, below = lax.rem(lev + 1, levs), lax.rem(lev + levs - 1, levs)

    weights = [
        pltpu.make_async_copy(src, dst, w_sem.at[n])
        for n, (src, dst) in enumerate(((wq_hbm, wq), (wk_hbm, wk), (wv_hbm, wv), (wm_hbm, wm)))
    ]
    for copy in weights:
        copy.start()

    barrier = pltpu.get_barrier_semaphore()
    partners = [(east, lev), (west, lev), (east, above), (east, below), (west, above), (west, below)]
    partners += [(tile, lax.rem(lev + d, levs)) for d in range(1, levs)]
    for partner in partners:
        pl.semaphore_signal(barrier, inc=1, device_id=partner, device_id_type=MESH)

    def slab(ref, x, f=0):
        return ref[pl.ds(f * KL * ROWS + x, KL, stride=ROWS), :]

    def level(ref, k, f=0):
        return ref[(f * KL + k) * ROWS : (f * KL + k + 1) * ROWS, :]

    top = KL - 1
    up0_s[...] = jnp.concatenate(
        [slab(state, 3, 0), slab(state, 3, 1), slab(coef_x, 3), slab(slope, 3)], axis=0
    )
    kup0_s[...] = jnp.concatenate([level(state, top, 0), level(state, top, 3), level(coef_z, top)], axis=0)

    def halo_copies(n):
        routes = (
            (up0_s if n == 0 else up_s.at[n - 1], up0_r if n == 0 else up_r.at[n - 1], (east, lev)),
            (dn_s.at[n], dn_r.at[n], (west, lev)),
            (kup0_s if n == 0 else kup_s.at[n - 1], kup0_r if n == 0 else kup_r.at[n - 1], (tile, above)),
            (kdn_s.at[n], kdn_r.at[n], (tile, below)),
            (cu_s.at[n], cu_r.at[n], (east, above)),
            (cd_s.at[n], cd_r.at[n], (east, below)),
        )
        return [
            pltpu.make_async_remote_copy(
                src_ref=src, dst_ref=dst, send_sem=halo_ss.at[n, i], recv_sem=halo_rs.at[n, i],
                device_id=where, device_id_type=MESH,
            )
            for i, (src, dst, where) in enumerate(routes)
        ]

    def send_pressure(n, p):
        if n > 0:
            up_s[n - 1] = p[3]
            kup_s[n - 1] = jnp.concatenate([a[top:] for a in p], axis=0)
        dn_s[n] = p[0]
        kdn_s[n] = jnp.concatenate([a[0:1] for a in p], axis=0)
        cu_s[n] = p[3][top:]
        cd_s[n] = p[3][0:1]

    p = [slab(state, x, 0) for x in range(ROWS)]
    send_pressure(0, p)
    pl.semaphore_wait(barrier, len(partners))
    copies = halo_copies(0)
    for copy in copies:
        copy.start()

    in_west = (tile > 0).astype(F32)
    in_east = (tile < tiles - 1).astype(F32)
    in_below = (lev > 0).astype(F32)
    in_above = (lev < levs - 1).astype(F32)

    for copy in weights:
        copy.wait()
    m_level = lax.broadcasted_iota(jnp.int32, (LEVELS, CELLS), 0)
    bias[...] = jnp.where(m_level >= ground[pl.ds(lev, 1), :], 0.0, -1e30)
    prepare_maps(w_in, table, gain_attn, wq, wk, wv, wm, gain_head, w_tend, temper, lk, ls, lf, tcol)

    u = [None] + [slab(state, x, 1) for x in range(ROWS)]
    v = [slab(state, x, 2) for x in range(ROWS)]
    w = [slab(state, x, 3) for x in range(ROWS)]
    cx = [None] + [slab(coef_x, x) for x in range(ROWS)]
    sl = [None] + [slab(slope, x) for x in range(ROWS)]
    cy = [slab(coef_y, x) for x in range(ROWS)]
    cz = [slab(coef_z, x) for x in range(ROWS)]
    cp = [slab(compress, x) for x in range(ROWS)]
    w_lo = cz_lo = None
    for n in range(3):
        for copy in copies:
            copy.wait()
        if n == 0:
            west_p = up0_r[0:KL] * in_west
            u[0] = up0_r[KL : 2 * KL] * in_west
            cx[0] = up0_r[2 * KL : 3 * KL] * in_west
            sl[0] = up0_r[3 * KL : 4 * KL] * in_west
            low = kup0_r[...] * in_below
            p_lo = [low[x : x + 1] for x in range(ROWS)]
            w_lo = [low[ROWS + x : ROWS + x + 1] for x in range(ROWS)]
            cz_lo = [low[2 * ROWS + x : 2 * ROWS + x + 1] for x in range(ROWS)]
        else:
            west_p = up_r[n - 1] * in_west
            low = kup_r[n - 1] * in_below
            p_lo = [low[x : x + 1] for x in range(ROWS)]
        high = kdn_r[n] * in_above
        p_lo = [cu_r[n] * (in_west * in_below)] + p_lo
        p_hi = [cd_r[n] * (in_west * in_above)] + [high[x : x + 1] for x in range(ROWS)]
        east_p = dn_r[n] * in_east
        p, u, v, w, w_lo = substep([west_p] + p + [east_p], p_lo, p_hi, u, v, w, w_lo, cx, sl, cy, cz, cz_lo, cp)
        if n < 2:
            send_pressure(n + 1, p)
            copies = halo_copies(n + 1)
            for copy in copies:
                copy.start()

    for x in range(ROWS):
        fields = jnp.concatenate([p[x], u[x + 1], v[x], w[x]], axis=0)
        cur[x] = fields
        feat_s[x] = fields.astype(BF16).astype(F32)

    def feature_copy(d):
        to = lax.rem(lev + d, levs)
        return pltpu.make_async_remote_copy(
            src_ref=feat_s.at[to], dst_ref=feat_r.at[lev], send_sem=feat_ss.at[d - 1], recv_sem=feat_rs.at[d - 1],
            device_id=(tile, to), device_id_type=MESH,
        )

    sends = [feature_copy(d) for d in range(1, levs)]
    for copy in sends:
        copy.start()
    fl[...] = jnp.zeros_like(fl)
    feat_r[lev] = feat_s[lev]
    for copy in sends:
        copy.wait()
    for s in range(levs):
        for f in range(4):
            a = feat_r[s, KL * f : KL * f + KL]
            fm[f, KL * s : KL * s + KL] = a
            fl[KL * s : KL * s + KL, f, :] = a

    @pl.loop(0, LEVELS, step=4)
    def _(l):
        for b in range(4):
            key_pass(l + b, fl, lk, rk, rs, eq)

    def tendency_copy(d):
        to = lax.rem(lev + d, levs)
        return pltpu.make_async_remote_copy(
            src_ref=tend_s.at[to], dst_ref=tend_r.at[lev], send_sem=tend_ss.at[d - 1], recv_sem=tend_rs.at[d - 1],
            device_id=(tile, to), device_id_type=MESH,
        )

    for d in range(1, levs + 1):
        to = lax.rem(lev + d, levs)

        @pl.loop(0, KL, step=2)
        def _(k):
            query_pass(to * KL + k, fl, fm, bias, ls, lf, tcol, rk, rs, eq, ot)

        for f in range(4):
            tend_s[to, KL * f : KL * f + KL] = ot[pl.ds(pl.multiple_of(to * KL, KL), KL), f, :]
        if d < levs:
            tendency_copy(d).start()

    tend_r[lev] = tend_s[lev]
    for d in range(1, levs):
        tendency_copy(d).wait()
    for x in range(ROWS):
        for f in range(4):
            rows = slice(KL * f, KL * f + KL)
            out[pl.ds(f * KL * ROWS + x, KL, stride=ROWS), :] = cur[x, rows] + tend_r[x, rows]


def shards(state, coef_x, coef_y, coef_z, slope, compress, ground, w_in, level_table, gain_attn,
           w_query, w_key, w_value, w_mix, temper, gain_head, w_tend):
    tiles, levs = lax.axis_size("tile"), lax.axis_size("lev")
    vmem = pl.BlockSpec(memory_space=pltpu.VMEM)
    smem = pl.BlockSpec(memory_space=pltpu.SMEM)
    hbm = pl.BlockSpec(memory_space=pl.ANY)
    dma = pltpu.SemaphoreType.DMA

    def buf(*shape, dtype=F32):
        return pltpu.VMEM(shape, dtype)

    def pair(*shape):
        return [buf(*shape), buf(*shape)]

    flat = KL * ROWS
    result = pl.pallas_call(
        lambda *refs: whole(tiles, levs, *refs),
        out_shape=jax.ShapeDtypeStruct((4 * flat, CELLS), F32),
        in_specs=[vmem] * 7 + [smem] + [vmem] * 5 + [hbm] * 4,
        out_specs=vmem,
        scratch_shapes=[
            buf(LEVELS, 8, CELLS), buf(LEVELS, 8, CELLS),
            buf(48, 128, dtype=BF16), buf(368, 128, dtype=BF16), buf(528, 640, dtype=BF16),
            buf(8, 128), buf(HEADS, LEVELS, CELLS), buf(LEVELS, CELLS), buf(LEVELS, CELLS), buf(LEVELS, CELLS),
            buf(4, LEVELS, CELLS),
            *[buf(WIDTH, WIDTH, dtype=BF16)] * 4, dma((4,)),
            *pair(4 * KL, CELLS), *pair(2, KL, CELLS), *pair(3, KL, CELLS),
            *pair(3 * ROWS, CELLS), *pair(2, ROWS, CELLS), *pair(3, ROWS, CELLS),
            *pair(3, 1, CELLS), *pair(3, 1, CELLS), dma((3, 6)), dma((3, 6)),
            *pair(levs, 4 * KL, CELLS), dma((levs - 1,)), dma((levs - 1,)),
            *pair(levs, 4 * KL, CELLS), dma((levs - 1,)), dma((levs - 1,)),
            buf(ROWS, 4 * KL, CELLS),
        ],
        compiler_params=pltpu.CompilerParams(
            collective_id=0, has_side_effects=True, vmem_limit_bytes=40 * 2**20
        ),
        name="substeps_and_columns",
    )(state.reshape(4 * flat, CELLS), *[a.reshape(flat, CELLS) for a in (coef_x, coef_y, coef_z, slope, compress)],
      ground, temper, w_in, level_table, gain_attn.reshape(1, WIDTH), gain_head.reshape(1, WIDTH), w_tend.T,
      w_query, w_key, w_value, w_mix)
    return result.reshape(4, KL, ROWS, CELLS)


def solution(mesh):
    block = P("lev", "tile", None)
    placed = (P(None, "lev", "tile", None),) + (block,) * 5 + (P("tile", None),) + (P(),) * 10
    return jax.shard_map(
        shards, mesh=mesh, in_specs=placed, out_specs=P(None, "lev", "tile", None), check_vma=False
    )
```

```python
import math

import jax
import jax.numpy as jnp
from jax import lax
from jax.experimental import pallas as pl
from jax.experimental.pallas import tpu as pltpu
from jax.sharding import PartitionSpec as P

EPS = 1e-6
F32, BF16 = jnp.float32, jnp.bfloat16
LOG2E = math.log2(math.e)
HEADS, WIDTH, LEVELS, CELLS = 8, 512, 32, 128
HS = WIDTH // HEADS
X = 40


def dot(a, b):
    return jnp.dot(a, b, preferred_element_type=F32)


def dot_t(a, b):
    return lax.dot_general(a, b, (((1,), (1,)), ((), ())), precision=lax.Precision.HIGHEST, preferred_element_type=F32)


def split3(a):
    hi = a.astype(BF16).astype(F32)
    mid = (a - hi).astype(BF16).astype(F32)
    return hi, mid, a - hi - mid


def spread(a):
    hi, mid, lo = split3(a)
    return (hi + pltpu.roll(mid, X, 1) + pltpu.roll(lo, 2 * X, 1)).astype(BF16)


def prepare_maps(w_in, table, gain_attn, wq, wk, wv, wm, gain_head, w_tend, temper, lk, ls, lf, tcol):
    emb = jnp.concatenate([w_in[...].astype(F32), jnp.zeros((4, WIDTH), F32), table[...]], axis=0)
    xg3 = jnp.concatenate(split3(emb * gain_attn[...]), axis=0).astype(BF16)

    def through(w):
        a = dot(xg3, w[...])
        return a[:X] + a[X : 2 * X] + a[2 * X :]

    aq, ak, av = through(wq), through(wk), through(wv)
    pad = jnp.zeros((128 - X, WIDTH), F32)
    aq_p = jnp.concatenate([aq, pad], axis=0)
    ak_p = jnp.concatenate([ak, pad], axis=0)
    head = lax.broadcasted_iota(jnp.int32, (X, WIDTH), 1) // HS

    def by_head(a):
        return jnp.concatenate([jnp.where(head == h, a, 0.0) for h in range(HEADS)], axis=0)

    kb = by_head(ak)
    qb = by_head(aq)
    s_map = dot_t(kb, aq_p)
    kk = dot_t(kb, ak_p)
    qq = dot_t(qb, aq_p)
    ee = dot_t(emb, jnp.concatenate([emb, pad], axis=0))
    lane = lax.broadcasted_iota(jnp.int32, (1, 128), 1)
    twice = jnp.where(lane < 8, 1.0, 2.0)
    r40 = lax.broadcasted_iota(jnp.int32, (X, 128), 0)
    l40 = lax.broadcasted_iota(jnp.int32, (X, 128), 1)
    diag = (r40 == l40) & (r40 >= 8)

    def norm_rows(g):
        return [g[i : i + 1] * twice for i in range(4)] + [jnp.sum(jnp.where(diag, g, 0.0), axis=0, keepdims=True)]

    def norm_map(gram):
        per = [norm_rows(gram[X * h : X * h + X]) for h in range(HEADS)]
        return jnp.concatenate([per[h][i] for i in range(5) for h in range(HEADS)], axis=0)

    e_rows = norm_rows(ee) + [jnp.zeros((3, 128), F32)]
    lk[...] = spread(jnp.concatenate([norm_map(kk)] + e_rows, axis=0))
    ls[0:320] = spread(s_map)
    ls[320:360] = spread(norm_map(qq))
    ls[360:368] = jnp.zeros((8, 128), BF16)

    vh, vm, _ = split3(by_head(av))
    c = dot(vh.astype(BF16), wm[...]) + dot(vm.astype(BF16), wm[...])
    eh, em, el = split3(emb)
    rows = [c[X * h + 8 : X * h + X] for h in range(HEADS)]
    rows += [jnp.broadcast_to(c[X * h + i : X * h + i + 1], (8, WIDTH)) for h in range(HEADS) for i in range(4)]
    rows += [eh, em, el, jnp.zeros((8, WIDTH), F32)]
    lft = jnp.concatenate(rows, axis=0)
    wt = jnp.concatenate([w_tend[...].astype(F32), jnp.zeros((12, WIDTH), F32)], axis=0) * gain_head[...]
    t = dot_t(wt, lft)
    th = t[:8].astype(BF16).astype(F32)
    lf[0:512] = lft.T.astype(BF16)
    lf[512:528] = jnp.concatenate([th, t[:8] - th], axis=0).astype(BF16)
    square = (HEADS, HEADS)
    on_diag = lax.broadcasted_iota(jnp.int32, square, 0) == lax.broadcasted_iota(jnp.int32, square, 1)
    scale = jnp.sum(jnp.where(on_diag, temper[...], 0.0), axis=1, keepdims=True) * (LOG2E / math.sqrt(HS))
    tcol[...] = jnp.broadcast_to(scale, (HEADS, 128))


def token_rows(fl, l):
    lev = lax.broadcasted_iota(jnp.int32, (LEVELS, CELLS), 0) == l
    one = jnp.concatenate([fl[l], lev.astype(F32)], axis=0)
    return jnp.concatenate([one, one, one, jnp.zeros((8, CELLS), F32)], axis=0).astype(BF16)


def norms_at(out, f, base, epsq, scale):
    n = out[base + 32 : base + 40]
    for i in range(4):
        n = n + f[i : i + 1] * out[base + 8 * i : base + 8 * i + 8]
    return lax.rsqrt(jnp.maximum(n, 0.0) * (1.0 / HS) + epsq) * scale


def key_pass(l, fl, lk, rk, rs, eq):
    out = dot(lk[...], token_rows(fl, l))
    f = fl[l]
    n = out[44:45]
    for i in range(4):
        n = n + f[i : i + 1] * out[40 + i : 41 + i]
    ms = jnp.maximum(n, 0.0) * (1.0 / WIDTH) + EPS
    rs[pl.ds(l, 1), :] = lax.rsqrt(ms)
    eq[pl.ds(l, 1), :] = EPS * ms
    rk[:, l, :] = norms_at(out, f, 0, EPS * ms, 1.0)


def query_pass(l0, fl, fm, bias, ls, lf, tcol, rk, rs, eq, ot):
    x = jnp.concatenate([token_rows(fl, l0), token_rows(fl, l0 + 1)], axis=1)
    out = dot(ls[...], x)
    parts = []
    for a in range(2):
        o = out[:, 128 * a : 128 * a + 128]
        rq = norms_at(o, fl[l0 + a], 320, eq[pl.ds(l0 + a, 1), :], tcol[...])
        probs, sums = [], []
        for h in range(HEADS):
            s = o[X * h + 8 : X * h + X]
            for i in range(4):
                s = s + fm[i] * o[X * h + i : X * h + i + 1]
            s = s * rk[h] * rq[h : h + 1] + bias[...]
            p = jnp.exp2(s - jnp.max(s, axis=0, keepdims=True))
            p = p * (1.0 / jnp.sum(p, axis=0, keepdims=True)) * rs[...]
            probs.append(p)
            for i in range(4):
                z = p * fm[i]
                sums.append(z[0:8] + z[8:16] + z[16:24] + z[24:32])
        parts.append(jnp.concatenate(probs + sums, axis=0).astype(BF16))
    rhs = jnp.concatenate([jnp.concatenate(parts, axis=1), x], axis=0)
    fin = dot(lf[...], rhs)
    stream = fin[:512]
    ms = jnp.mean(stream * stream, axis=0, keepdims=True)
    tend = (fin[512:520] + fin[520:528]) * lax.rsqrt(ms + EPS)
    ot[l0] = tend[:, :128]
    ot[l0 + 1] = tend[:, 128:]


ROWS = 4
KL = 8
MESH = pl.DeviceIdType.MESH


NAMES = ("p", "u", "v", "w", "cx", "cy", "cz", "sl", "cp")
EASTWARD = [(n, x) for n in NAMES for x in range(1 if n in ("p", "u", "cx", "sl") else 2, ROWS)]
WESTWARD = [(n, x) for n in NAMES for x in range(3 if n == "p" else 2)]
HALF = KL // 2
ROUTES = [(dx, dk) for dx in (1, -1, 0) for dk in (0, 1, -1) if (dx, dk) != (0, 0)]


def message_rows(dx, dk):
    if dx == 0:
        return len(NAMES) * HALF * ROWS
    slabs = len(EASTWARD if dx > 0 else WESTWARD)
    return -(-slabs * (HALF if dk else KL) // 16) * 16


def substep(n, p, u, v, w, cx, sl, cy, cz, cp):
    up = {x: pltpu.roll(a, 3 * KL - 1, 0) for x, a in p.items()}
    down = {x: pltpu.roll(a, 1, 0) for x, a in p.items()}
    u = {
        x: u[x] - cx[x] * (p[x + 1] - p[x]) - 0.5 * sl[x] * (up[x] - down[x])
        for x in range(n - 3, ROWS + 2 - n)
    }
    new_p, new_v, new_w = {}, {}, {}
    for x in range(n - 2, ROWS + 2 - n):
        c = p[x]
        wx = w[x] - cz[x] * (up[x] - c)
        vx = v[x] - cy[x] * (pltpu.roll(c, CELLS - 1, 1) - c)
        div = (u[x] - u[x - 1]) + (vx - pltpu.roll(vx, 1, 1)) + (wx - pltpu.roll(wx, 1, 0))
        new_p[x] = c - cp[x] * div
        new_v[x] = vx
        new_w[x] = wx
    return new_p, u, new_v, new_w


def whole(tiles, levs, *refs):
    hbm, out, held, in_sem, rest = refs[:17], refs[17], refs[18:35], refs[35], refs[36:]
    loads = [pltpu.make_async_copy(src, dst, in_sem.at[n]) for n, (src, dst) in enumerate(zip(hbm, held))]
    for copy in loads:
        copy.start()
    (state, coef_x, coef_y, coef_z, slope, compress, ground, temper, w_in, table, gain_attn, gain_head, w_tend,
     wq, wk, wv, wm) = held
    (fl, ot, lk, ls, lf, tcol, rk, rs, eq, bias, fm,
     halo_ss, halo_rs, feat_s, feat_r, feat_ss, feat_rs, tend_s, tend_r, tend_ss, tend_rs, cur) = rest[:22]
    halo_s, halo_r, wide = rest[22:30], rest[30:38], rest[38:46]
    tile, lev = lax.axis_index("tile"), lax.axis_index("lev")
    there = [
        (tile + dx >= 0) & (tile + dx < tiles) & (lev + dk >= 0) & (lev + dk < levs) for dx, dk in ROUTES
    ]
    source_there = [there[ROUTES.index((-dx, -dk))] for dx, dk in ROUTES]

    barrier = pltpu.get_barrier_semaphore()
    for d in range(1, levs):
        pl.semaphore_signal(barrier, inc=1, device_id=(tile, lax.rem(lev + d, levs)), device_id_type=MESH)
    for (dx, dk), exists in zip(ROUTES, there):
        if dx:
            @pl.when(exists)
            def _():
                pl.semaphore_signal(barrier, inc=1, device_id=(tile + dx, lev + dk), device_id_type=MESH)

    for copy in loads[:6]:
        copy.wait()
    held_by = dict(zip(NAMES, [(state, f) for f in range(4)] + [(a, 0) for a in (coef_x, coef_y, coef_z, slope, compress)]))

    def slab(name, x, k=0, count=KL):
        ref, f = held_by[name]
        return ref[pl.ds((f * KL + k) * ROWS + x, count, stride=ROWS), :]

    for i, (dx, dk) in enumerate(ROUTES):
        k = HALF if dk > 0 else 0
        if dx == 0:
            pieces = [ref[(f * KL + k) * ROWS : (f * KL + k + HALF) * ROWS, :] for ref, f in held_by.values()]
        else:
            pieces = [slab(n, x, k, HALF if dk else KL) for n, x in (EASTWARD if dx > 0 else WESTWARD)]
        extra = message_rows(dx, dk) - sum(a.shape[0] for a in pieces)
        if extra:
            pieces.append(jnp.zeros((extra, CELLS), F32))
        halo_s[i][...] = jnp.concatenate(pieces, axis=0).astype(BF16)

        @pl.when(jnp.logical_not(source_there[i]))
        def _():
            halo_r[i][...] = jnp.zeros_like(halo_r[i])

    def halo_copy(i):
        dx, dk = ROUTES[i]
        return pltpu.make_async_remote_copy(
            src_ref=halo_s[i], dst_ref=halo_r[i], send_sem=halo_ss.at[i], recv_sem=halo_rs.at[i],
            device_id=(tile + dx, lev + dk), device_id_type=MESH,
        )

    beside = [exists.astype(jnp.int32) for (dx, dk), exists in zip(ROUTES, there) if dx]
    pl.semaphore_wait(barrier, levs - 1 + sum(beside))
    for i, exists in enumerate(there):
        @pl.when(exists)
        def _():
            halo_copy(i).start()

    for copy in loads[6:]:
        copy.wait()
    m_level = lax.broadcasted_iota(jnp.int32, (LEVELS, CELLS), 0)
    bias[...] = jnp.where(m_level >= ground[pl.ds(lev, 1), :], 0.0, -1e30)
    prepare_maps(w_in, table, gain_attn, wq, wk, wv, wm, gain_head, w_tend, temper, lk, ls, lf, tcol)

    for i in range(len(ROUTES)):
        @pl.when(there[i])
        def _():
            halo_copy(i).wait_send()

        @pl.when(source_there[i])
        def _():
            halo_copy(i).wait_recv()

    got = {}
    for i, (dx, dk) in enumerate(ROUTES):
        rows = message_rows(dx, dk)
        wide[i][0:16] = jnp.zeros((16, CELLS), F32)
        wide[i][16 : 16 + rows] = halo_r[i][...].astype(F32)
        wide[i][16 + rows :] = jnp.zeros((16, CELLS), F32)
        got[dx, dk] = wide[i]

    def column(a, name, x):
        if 0 <= x < ROWS:
            mid = slab(name, x)
            at = 16 + HALF * ROWS * a + x
            lo = got[0, 1][pl.ds(at - HALF * ROWS, KL, stride=ROWS), :]
            hi = got[0, -1][pl.ds(at, KL, stride=ROWS), :]
        else:
            dx = 1 if x < 0 else -1
            n = (EASTWARD if x < 0 else WESTWARD).index((name, x + ROWS if x < 0 else x - ROWS))
            mid = got[dx, 0][16 + KL * n : 16 + KL * n + KL, :]
            lo = got[dx, 1][16 + HALF * (n - 1) : 16 + HALF * (n + 1), :]
            hi = got[dx, -1][16 + HALF * n : 16 + HALF * (n + 2), :]
        return jnp.concatenate([lo, mid, hi], axis=0)

    held_x = {n: [x for x in range(-3, 7) if 0 <= x < ROWS or (n, x + ROWS) in EASTWARD and x < 0 or (n, x - ROWS) in WESTWARD and x >= ROWS] for n in NAMES}
    field = {n: {x: column(a, n, x) for x in held_x[n]} for a, n in enumerate(NAMES)}
    p, u, v, w = field["p"], field["u"], field["v"], field["w"]
    for n in range(3):
        p, u, v, w = substep(n, p, u, v, w, *[field[m] for m in ("cx", "sl", "cy", "cz", "cp")])

    mid = slice(KL, 2 * KL)
    for x in range(ROWS):
        fields = jnp.concatenate([a[x][mid] for a in (p, u, v, w)], axis=0)
        cur[x] = fields
        feat_s[x] = fields.astype(BF16).astype(F32)

    def feature_copy(d):
        to = lax.rem(lev + d, levs)
        return pltpu.make_async_remote_copy(
            src_ref=feat_s.at[to], dst_ref=feat_r.at[lev], send_sem=feat_ss.at[d - 1], recv_sem=feat_rs.at[d - 1],
            device_id=(tile, to), device_id_type=MESH,
        )

    sends = [feature_copy(d) for d in range(1, levs)]
    for copy in sends:
        copy.start()
    fl[...] = jnp.zeros_like(fl)
    feat_r[lev] = feat_s[lev]
    with jax.named_scope("features_wait"):
        for copy in sends:
            copy.wait()
    for s in range(levs):
        for f in range(4):
            a = feat_r[s, KL * f : KL * f + KL]
            fm[f, KL * s : KL * s + KL] = a
            fl[KL * s : KL * s + KL, f, :] = a

    with jax.named_scope("keys"):
        @pl.loop(0, LEVELS, step=4)
        def _(l):
            for b in range(4):
                key_pass(l + b, fl, lk, rk, rs, eq)

    def tendency_copy(d):
        to = lax.rem(lev + d, levs)
        return pltpu.make_async_remote_copy(
            src_ref=tend_s.at[to], dst_ref=tend_r.at[lev], send_sem=tend_ss.at[d - 1], recv_sem=tend_rs.at[d - 1],
            device_id=(tile, to), device_id_type=MESH,
        )

    with jax.named_scope("queries"):
        for d in range(1, levs + 1):
            to = lax.rem(lev + d, levs)

            @pl.loop(0, KL, step=2)
            def _(k):
                query_pass(to * KL + k, fl, fm, bias, ls, lf, tcol, rk, rs, eq, ot)

            for f in range(4):
                tend_s[to, KL * f : KL * f + KL] = ot[pl.ds(pl.multiple_of(to * KL, KL), KL), f, :]
            if d < levs:
                tendency_copy(d).start()

    tend_r[lev] = tend_s[lev]
    with jax.named_scope("tendency_wait"):
        for d in range(1, levs):
            tendency_copy(d).wait()
    for x in range(ROWS):
        for f in range(4):
            rows = slice(KL * f, KL * f + KL)
            out[pl.ds(f * KL * ROWS + x, KL, stride=ROWS), :] = cur[x, rows] + tend_r[x, rows]


def shards(state, coef_x, coef_y, coef_z, slope, compress, ground, w_in, level_table, gain_attn,
           w_query, w_key, w_value, w_mix, temper, gain_head, w_tend):
    tiles, levs = lax.axis_size("tile"), lax.axis_size("lev")
    dma = pltpu.SemaphoreType.DMA

    def buf(*shape, dtype=F32):
        return pltpu.VMEM(shape, dtype)

    def pair(*shape):
        return [buf(*shape), buf(*shape)]

    flat = KL * ROWS
    operands = (
        state.reshape(4 * flat, CELLS), *[a.reshape(flat, CELLS) for a in (coef_x, coef_y, coef_z, slope, compress)],
        ground, temper.reshape(1, HEADS), w_in, level_table, gain_attn.reshape(1, WIDTH), gain_head.reshape(1, WIDTH),
        w_tend.T, w_query, w_key, w_value, w_mix,
    )
    result = pl.pallas_call(
        lambda *refs: whole(tiles, levs, *refs),
        out_shape=jax.ShapeDtypeStruct((4 * flat, CELLS), F32),
        in_specs=[pl.BlockSpec(memory_space=pl.ANY)] * len(operands),
        out_specs=pl.BlockSpec(memory_space=pltpu.VMEM),
        scratch_shapes=[
            *[buf(*a.shape, dtype=a.dtype) for a in operands], dma((len(operands),)),
            buf(LEVELS, 8, CELLS), buf(LEVELS, 8, CELLS),
            buf(48, 128, dtype=BF16), buf(368, 128, dtype=BF16), buf(528, 640, dtype=BF16),
            buf(8, 128), buf(HEADS, LEVELS, CELLS), buf(LEVELS, CELLS), buf(LEVELS, CELLS), buf(LEVELS, CELLS),
            buf(4, LEVELS, CELLS),
            dma((len(ROUTES),)), dma((len(ROUTES),)),
            *pair(levs, 4 * KL, CELLS), dma((levs - 1,)), dma((levs - 1,)),
            *pair(levs, 4 * KL, CELLS), dma((levs - 1,)), dma((levs - 1,)),
            buf(ROWS, 4 * KL, CELLS),
            *[buf(message_rows(*r), CELLS, dtype=BF16) for r in ROUTES] * 2,
            *[buf(message_rows(*r) + 32, CELLS) for r in ROUTES],
        ],
        compiler_params=pltpu.CompilerParams(
            collective_id=0, has_side_effects=True, vmem_limit_bytes=60 * 2**20
        ),
        name="substeps_and_columns",
    )(*operands)
    return result.reshape(4, KL, ROWS, CELLS)


def solution(mesh):
    block = P("lev", "tile", None)
    placed = (P(None, "lev", "tile", None),) + (block,) * 5 + (P("tile", None),) + (P(),) * 10
    return jax.shard_map(
        shards, mesh=mesh, in_specs=placed, out_specs=P(None, "lev", "tile", None), check_vma=False
    )
```

```python
import math

import jax
import jax.numpy as jnp
from jax import lax
from jax.experimental import pallas as pl
from jax.experimental.pallas import tpu as pltpu
from jax.sharding import PartitionSpec as P

EPS = 1e-6
F32, BF16 = jnp.float32, jnp.bfloat16
LOG2E = math.log2(math.e)
HEADS, WIDTH, LEVELS, CELLS = 8, 512, 32, 128
HS = WIDTH // HEADS
X = 40


def dot(a, b):
    return jnp.dot(a, b, preferred_element_type=F32)


def dot_t(a, b):
    return lax.dot_general(a, b, (((1,), (1,)), ((), ())), precision=lax.Precision.HIGHEST, preferred_element_type=F32)


def split3(a):
    hi = a.astype(BF16).astype(F32)
    mid = (a - hi).astype(BF16).astype(F32)
    return hi, mid, a - hi - mid


def spread(a):
    hi, mid, lo = split3(a)
    return (hi + pltpu.roll(mid, X, 1) + pltpu.roll(lo, 2 * X, 1)).astype(BF16)


def prepare_maps(w_in, table, gain_attn, wq, wk, wv, wm, gain_head, w_tend, temper, lk, ls, lf, tcol):
    emb = jnp.concatenate([w_in[...].astype(F32), jnp.zeros((4, WIDTH), F32), table[...]], axis=0)
    xg3 = jnp.concatenate(split3(emb * gain_attn[...]), axis=0).astype(BF16)

    def through(w):
        a = dot(xg3, w[...])
        return a[:X] + a[X : 2 * X] + a[2 * X :]

    aq, ak, av = through(wq), through(wk), through(wv)
    pad = jnp.zeros((128 - X, WIDTH), F32)
    aq_p = jnp.concatenate([aq, pad], axis=0)
    ak_p = jnp.concatenate([ak, pad], axis=0)
    head = lax.broadcasted_iota(jnp.int32, (X, WIDTH), 1) // HS

    def by_head(a):
        return jnp.concatenate([jnp.where(head == h, a, 0.0) for h in range(HEADS)], axis=0)

    kb = by_head(ak)
    qb = by_head(aq)
    s_map = dot_t(kb, aq_p)
    kk = dot_t(kb, ak_p)
    qq = dot_t(qb, aq_p)
    ee = dot_t(emb, jnp.concatenate([emb, pad], axis=0))
    lane = lax.broadcasted_iota(jnp.int32, (1, 128), 1)
    twice = jnp.where(lane < 8, 1.0, 2.0)
    r40 = lax.broadcasted_iota(jnp.int32, (X, 128), 0)
    l40 = lax.broadcasted_iota(jnp.int32, (X, 128), 1)
    diag = (r40 == l40) & (r40 >= 8)

    def norm_rows(g):
        return [g[i : i + 1] * twice for i in range(4)] + [jnp.sum(jnp.where(diag, g, 0.0), axis=0, keepdims=True)]

    def norm_map(gram):
        per = [norm_rows(gram[X * h : X * h + X]) for h in range(HEADS)]
        return jnp.concatenate([per[h][i] for i in range(5) for h in range(HEADS)], axis=0)

    e_rows = norm_rows(ee) + [jnp.zeros((3, 128), F32)]
    lk[...] = spread(jnp.concatenate([norm_map(kk)] + e_rows, axis=0))
    ls[0:320] = spread(s_map)
    ls[320:360] = spread(norm_map(qq))
    ls[360:368] = jnp.zeros((8, 128), BF16)

    vh, vm, _ = split3(by_head(av))
    c = dot(vh.astype(BF16), wm[...]) + dot(vm.astype(BF16), wm[...])
    eh, em, el = split3(emb)
    rows = [c[X * h + 8 : X * h + X] for h in range(HEADS)]
    rows += [jnp.broadcast_to(c[X * h + i : X * h + i + 1], (4, WIDTH)) for h in range(HEADS) for i in range(4)]
    rows += [eh, em, el, jnp.zeros((8, WIDTH), F32)]
    lft = jnp.concatenate(rows, axis=0)
    wt = jnp.concatenate([w_tend[...].astype(F32), jnp.zeros((12, WIDTH), F32)], axis=0) * gain_head[...]
    t = dot_t(wt, lft)
    th = t[:8].astype(BF16).astype(F32)
    lf[0:512] = lft.T.astype(BF16)
    lf[512:528] = jnp.concatenate([th, t[:8] - th], axis=0).astype(BF16)
    square = (HEADS, HEADS)
    on_diag = lax.broadcasted_iota(jnp.int32, square, 0) == lax.broadcasted_iota(jnp.int32, square, 1)
    scale = jnp.sum(jnp.where(on_diag, temper[...], 0.0), axis=1, keepdims=True) * (LOG2E / math.sqrt(HS))
    tcol[...] = jnp.broadcast_to(scale, (HEADS, 128))


def token_rows(fl, l):
    lev = lax.broadcasted_iota(jnp.int32, (LEVELS, CELLS), 0) == l
    one = jnp.concatenate([fl[l], lev.astype(F32)], axis=0)
    return jnp.concatenate([one, one, one, jnp.zeros((8, CELLS), F32)], axis=0).astype(BF16)


def norms_at(out, f, base, epsq, scale):
    n = out[base + 32 : base + 40]
    for i in range(4):
        n = n + f[i : i + 1] * out[base + 8 * i : base + 8 * i + 8]
    return lax.rsqrt(jnp.maximum(n, 0.0) * (1.0 / HS) + epsq) * scale


def key_chunk(base, pairs, fl, lk, rk, rs, eq):
    for l0 in [base + 2 * j for j in range(pairs)]:
        x = jnp.concatenate([token_rows(fl, l0), token_rows(fl, l0 + 1)], axis=1)
        both = dot(lk[...], x)
        for a in range(2):
            l = l0 + a
            out = both[:, 128 * a : 128 * a + 128]
            f = fl[l]
            n = out[44:45]
            for i in range(4):
                n = n + f[i : i + 1] * out[40 + i : 41 + i]
            ms = jnp.maximum(n, 0.0) * (1.0 / WIDTH) + EPS
            rs[pl.ds(l, 1), :] = lax.rsqrt(ms)
            eq[pl.ds(l, 1), :] = EPS * ms
            rk[:, l, :] = norms_at(out, f, 0, EPS * ms, 1.0)


def score_terms(l0, fl, ls):
    x = jnp.concatenate([token_rows(fl, l0), token_rows(fl, l0 + 1)], axis=1)
    return x, dot(ls[...], x)


def attend(l0, x, out, fl, fm, bias, tcol, rk, rs, eq):
    parts = []
    low = lax.broadcasted_iota(jnp.int32, (8, CELLS), 0) < 4
    for a in range(2):
        o = out[:, 128 * a : 128 * a + 128]
        rq = norms_at(o, fl[l0 + a], 320, eq[pl.ds(l0 + a, 1), :], tcol[...])
        probs, sums = [], []
        for h in range(HEADS):
            s = o[X * h + 8 : X * h + X]
            for i in range(4):
                s = s + fm[i] * o[X * h + i : X * h + i + 1]
            s = s * rk[h] * rq[h : h + 1] + bias[...]
            p = jnp.exp2(s - jnp.max(s, axis=0, keepdims=True))
            p = p * (1.0 / jnp.sum(p, axis=0, keepdims=True)) * rs[...]
            probs.append(p)
            z = [p * fm[i] for i in range(4)]
            z = [a[0:8] + a[8:16] + a[16:24] + a[24:32] for a in z]
            for i in (0, 2):
                sums.append(jnp.where(low, z[i], z[i + 1]) + pltpu.roll(jnp.where(low, z[i + 1], z[i]), 4, 0))
        parts.append(jnp.concatenate(probs + sums, axis=0).astype(BF16))
    return jnp.concatenate([jnp.concatenate(parts, axis=1), x], axis=0)


def finish(l0, rhs, lf, ot):
    fin = dot(lf[...], rhs)
    stream = fin[:512]
    ms = jnp.mean(stream * stream, axis=0, keepdims=True)
    tend = (fin[512:520] + fin[520:528]) * lax.rsqrt(ms + EPS)
    ot[l0] = tend[:, :128]
    ot[l0 + 1] = tend[:, 128:]


def query_pairs(levels, fl, fm, bias, ls, lf, tcol, rk, rs, eq, ot, done=lambda n: None):
    pairs = len(levels)
    first, second = {}, {}
    for step in range(pairs + 2):
        if step < pairs:
            first[step] = score_terms(levels[step], fl, ls)
        if step >= 2:
            finish(levels[step - 2], second.pop(step - 2), lf, ot)
            done(step - 2)
        if 1 <= step <= pairs:
            second[step - 1] = attend(levels[step - 1], *first.pop(step - 1), fl, fm, bias, tcol, rk, rs, eq)


ROWS = 4
KL = 8
MESH = pl.DeviceIdType.MESH


NAMES = ("p", "u", "v", "w", "cx", "cy", "cz", "sl", "cp")
EASTWARD = [(n, x) for n in NAMES for x in range(1 if n in ("p", "u", "cx", "sl") else 2, ROWS)]
WESTWARD = [(n, x) for n in NAMES for x in range(3 if n == "p" else 2)]
HALF = KL // 2
ROUTES = [(dx, dk) for dx in (1, -1, 0) for dk in (0, 1, -1) if (dx, dk) != (0, 0)]


def message_rows(dx, dk):
    if dx == 0:
        return len(NAMES) * HALF * ROWS
    slabs = len(EASTWARD if dx > 0 else WESTWARD)
    return -(-slabs * (HALF if dk else KL) // 16) * 16


def substep(n, p, u, v, w, cx, sl, cy, cz, cp):
    up = {x: pltpu.roll(a, 3 * KL - 1, 0) for x, a in p.items()}
    down = {x: pltpu.roll(a, 1, 0) for x, a in p.items()}
    u = {
        x: u[x] - cx[x] * (p[x + 1] - p[x]) - 0.5 * sl[x] * (up[x] - down[x])
        for x in range(n - 3, ROWS + 2 - n)
    }
    new_p, new_v, new_w = {}, {}, {}
    for x in range(n - 2, ROWS + 2 - n):
        c = p[x]
        wx = w[x] - cz[x] * (up[x] - c)
        vx = v[x] - cy[x] * (pltpu.roll(c, CELLS - 1, 1) - c)
        div = (u[x] - u[x - 1]) + (vx - pltpu.roll(vx, 1, 1)) + (wx - pltpu.roll(wx, 1, 0))
        new_p[x] = c - cp[x] * div
        new_v[x] = vx
        new_w[x] = wx
    return new_p, u, new_v, new_w


def whole(tiles, levs, *refs):
    hbm, out, held, in_sem, rest = refs[:17], refs[17], refs[18:35], refs[35], refs[36:]
    (state, coef_x, coef_y, coef_z, slope, compress, ground, temper, w_in, table, gain_attn, gain_head, w_tend,
     wq, wk, wv, wm) = held
    (fl, ot, lk, ls, lf, tcol, rk, rs, eq, bias, fm,
     halo_ss, halo_rs, feat_s, feat_r, feat_ss, feat_rs, tend_s, tend_r, tend_ss, tend_rs, cur) = rest[:22]
    halo_s, halo_r, wide = rest[22:30], rest[30:38], rest[38:46]
    tile, lev = lax.axis_index("tile"), lax.axis_index("lev")
    there = [
        (tile + dx >= 0) & (tile + dx < tiles) & (lev + dk >= 0) & (lev + dk < levs) for dx, dk in ROUTES
    ]
    source_there = [there[ROUTES.index((-dx, -dk))] for dx, dk in ROUTES]

    barrier = pltpu.get_barrier_semaphore()
    for d in range(1, levs):
        pl.semaphore_signal(barrier, inc=1, device_id=(tile, lax.rem(lev + d, levs)), device_id_type=MESH)
    for (dx, dk), exists in zip(ROUTES, there):
        if dx:
            @pl.when(exists)
            def _():
                pl.semaphore_signal(barrier, inc=1, device_id=(tile + dx, lev + dk), device_id_type=MESH)

    loads = [pltpu.make_async_copy(src, dst, in_sem.at[n]) for n, (src, dst) in enumerate(zip(hbm, held))]
    for copy in loads:
        copy.start()
    for copy in loads[:6]:
        copy.wait()
    held_by = dict(zip(NAMES, [(state, f) for f in range(4)] + [(a, 0) for a in (coef_x, coef_y, coef_z, slope, compress)]))

    def slab(name, x, k=0, count=KL):
        ref, f = held_by[name]
        return ref[pl.ds((f * KL + k) * ROWS + x, count, stride=ROWS), :]

    for i, (dx, dk) in enumerate(ROUTES):
        k = HALF if dk > 0 else 0
        if dx == 0:
            pieces = [ref[(f * KL + k) * ROWS : (f * KL + k + HALF) * ROWS, :] for ref, f in held_by.values()]
        else:
            pieces = [slab(n, x, k, HALF if dk else KL) for n, x in (EASTWARD if dx > 0 else WESTWARD)]
        extra = message_rows(dx, dk) - sum(a.shape[0] for a in pieces)
        if extra:
            pieces.append(jnp.zeros((extra, CELLS), F32))
        halo_s[i][...] = jnp.concatenate(pieces, axis=0).astype(BF16)

        @pl.when(jnp.logical_not(source_there[i]))
        def _():
            halo_r[i][...] = jnp.zeros_like(halo_r[i])

    def halo_copy(i):
        dx, dk = ROUTES[i]
        return pltpu.make_async_remote_copy(
            src_ref=halo_s[i], dst_ref=halo_r[i], send_sem=halo_ss.at[i], recv_sem=halo_rs.at[i],
            device_id=(tile + dx, lev + dk), device_id_type=MESH,
        )

    beside = [exists.astype(jnp.int32) for (dx, dk), exists in zip(ROUTES, there) if dx]
    pl.semaphore_wait(barrier, levs - 1 + sum(beside))
    for i, exists in enumerate(there):
        @pl.when(exists)
        def _():
            halo_copy(i).start()

    for copy in loads[6:]:
        copy.wait()
    m_level = lax.broadcasted_iota(jnp.int32, (LEVELS, CELLS), 0)
    bias[...] = jnp.where(m_level >= ground[pl.ds(lev, 1), :], 0.0, -1e30)
    prepare_maps(w_in, table, gain_attn, wq, wk, wv, wm, gain_head, w_tend, temper, lk, ls, lf, tcol)

    for i in range(len(ROUTES)):
        @pl.when(there[i])
        def _():
            halo_copy(i).wait_send()

        @pl.when(source_there[i])
        def _():
            halo_copy(i).wait_recv()

    got = {}
    for i, (dx, dk) in enumerate(ROUTES):
        rows = message_rows(dx, dk)
        wide[i][0:16] = jnp.zeros((16, CELLS), F32)
        wide[i][16 : 16 + rows] = halo_r[i][...].astype(F32)
        wide[i][16 + rows :] = jnp.zeros((16, CELLS), F32)
        got[dx, dk] = wide[i]

    def column(a, name, x):
        if 0 <= x < ROWS:
            mid = slab(name, x)
            at = 16 + HALF * ROWS * a + x
            lo = got[0, 1][pl.ds(at - HALF * ROWS, KL, stride=ROWS), :]
            hi = got[0, -1][pl.ds(at, KL, stride=ROWS), :]
        else:
            dx = 1 if x < 0 else -1
            n = (EASTWARD if x < 0 else WESTWARD).index((name, x + ROWS if x < 0 else x - ROWS))
            mid = got[dx, 0][16 + KL * n : 16 + KL * n + KL, :]
            lo = got[dx, 1][16 + HALF * (n - 1) : 16 + HALF * (n + 1), :]
            hi = got[dx, -1][16 + HALF * n : 16 + HALF * (n + 2), :]
        return jnp.concatenate([lo, mid, hi], axis=0)

    held_x = {n: [x for x in range(-3, 7) if 0 <= x < ROWS or (n, x + ROWS) in EASTWARD and x < 0 or (n, x - ROWS) in WESTWARD and x >= ROWS] for n in NAMES}
    field = {n: {x: column(a, n, x) for x in held_x[n]} for a, n in enumerate(NAMES)}
    p, u, v, w = field["p"], field["u"], field["v"], field["w"]
    for n in range(3):
        p, u, v, w = substep(n, p, u, v, w, *[field[m] for m in ("cx", "sl", "cy", "cz", "cp")])

    mid = slice(KL, 2 * KL)
    for x in range(ROWS):
        fields = jnp.concatenate([a[x][mid] for a in (p, u, v, w)], axis=0)
        cur[x] = fields
        feat_s[x] = fields.astype(BF16).astype(F32)

    def feature_copy(d):
        to = lax.rem(lev + d, levs)
        return pltpu.make_async_remote_copy(
            src_ref=feat_s.at[to], dst_ref=feat_r.at[lev], send_sem=feat_ss.at[d - 1], recv_sem=feat_rs.at[d - 1],
            device_id=(tile, to), device_id_type=MESH,
        )

    for d in range(1, levs):
        feature_copy(d).start()
    fl[...] = jnp.zeros_like(fl)

    def take(features, s):
        for f in range(4):
            a = features[KL * f : KL * f + KL]
            at = pl.ds(pl.multiple_of(s * KL, KL), KL)
            fm[f, at] = a
            fl[at, f, :] = a
        key_chunk(s * KL, KL // 2, fl, lk, rk, rs, eq)

    take(feat_s[lev], lev)
    for d in range(1, levs):
        s = lax.rem(lev + levs - d, levs)
        feature_copy(d).wait_recv()
        take(feat_r[s], s)

    def tendency_copy(d):
        to = lax.rem(lev + d, levs)
        return pltpu.make_async_remote_copy(
            src_ref=tend_s.at[to], dst_ref=tend_r.at[lev], send_sem=tend_ss.at[d - 1], recv_sem=tend_rs.at[d - 1],
            device_id=(tile, to), device_id_type=MESH,
        )

    blocks = [lax.rem(lev + d, levs) for d in range(1, levs + 1)]

    def done(n):
        d, j = n // (KL // 2), n % (KL // 2)
        if j == KL // 2 - 1:
            to = blocks[d]
            for f in range(4):
                tend_s[to, KL * f : KL * f + KL] = ot[pl.ds(pl.multiple_of(to * KL, KL), KL), f, :]
            if d < levs - 1:
                tendency_copy(d + 1).start()

    query_pairs(
        [to * KL + k for to in blocks for k in range(0, KL, 2)], fl, fm, bias, ls, lf, tcol, rk, rs, eq, ot, done
    )
    tend_r[lev] = tend_s[lev]
    for d in range(1, levs):
        feature_copy(d).wait_send()
        tendency_copy(d).wait()
    for x in range(ROWS):
        for f in range(4):
            rows = slice(KL * f, KL * f + KL)
            out[pl.ds(f * KL * ROWS + x, KL, stride=ROWS), :] = cur[x, rows] + tend_r[x, rows]


def shards(state, coef_x, coef_y, coef_z, slope, compress, ground, w_in, level_table, gain_attn,
           w_query, w_key, w_value, w_mix, temper, gain_head, w_tend):
    tiles, levs = lax.axis_size("tile"), lax.axis_size("lev")
    dma = pltpu.SemaphoreType.DMA

    def buf(*shape, dtype=F32):
        return pltpu.VMEM(shape, dtype)

    def pair(*shape):
        return [buf(*shape), buf(*shape)]

    flat = KL * ROWS
    operands = (
        state.reshape(4 * flat, CELLS), *[a.reshape(flat, CELLS) for a in (coef_x, coef_y, coef_z, slope, compress)],
        ground, temper.reshape(1, HEADS), w_in, level_table, gain_attn.reshape(1, WIDTH), gain_head.reshape(1, WIDTH),
        w_tend.T, w_query, w_key, w_value, w_mix,
    )
    result = pl.pallas_call(
        lambda *refs: whole(tiles, levs, *refs),
        out_shape=jax.ShapeDtypeStruct((4 * flat, CELLS), F32),
        in_specs=[pl.BlockSpec(memory_space=pl.ANY)] * len(operands),
        out_specs=pl.BlockSpec(memory_space=pltpu.VMEM),
        scratch_shapes=[
            *[buf(*a.shape, dtype=a.dtype) for a in operands], dma((len(operands),)),
            buf(LEVELS, 8, CELLS), buf(LEVELS, 8, CELLS),
            buf(48, 128, dtype=BF16), buf(368, 128, dtype=BF16), buf(528, 512, dtype=BF16),
            buf(8, 128), buf(HEADS, LEVELS, CELLS), buf(LEVELS, CELLS), buf(LEVELS, CELLS), buf(LEVELS, CELLS),
            buf(4, LEVELS, CELLS),
            dma((len(ROUTES),)), dma((len(ROUTES),)),
            *pair(levs, 4 * KL, CELLS), dma((levs - 1,)), dma((levs - 1,)),
            *pair(levs, 4 * KL, CELLS), dma((levs - 1,)), dma((levs - 1,)),
            buf(ROWS, 4 * KL, CELLS),
            *[buf(message_rows(*r), CELLS, dtype=BF16) for r in ROUTES] * 2,
            *[buf(message_rows(*r) + 32, CELLS) for r in ROUTES],
        ],
        compiler_params=pltpu.CompilerParams(
            collective_id=0, has_side_effects=True, vmem_limit_bytes=60 * 2**20
        ),
        name="substeps_and_columns",
    )(*operands)
    return result.reshape(4, KL, ROWS, CELLS)


def solution(mesh):
    block = P("lev", "tile", None)
    placed = (P(None, "lev", "tile", None),) + (block,) * 5 + (P("tile", None),) + (P(),) * 10
    return jax.shard_map(
        shards, mesh=mesh, in_specs=placed, out_specs=P(None, "lev", "tile", None), check_vma=False
    )
```

```python
import math

import jax
import jax.numpy as jnp
from jax import lax
from jax.experimental import pallas as pl
from jax.experimental.pallas import tpu as pltpu
from jax.sharding import PartitionSpec as P

EPS = 1e-6
F32, BF16 = jnp.float32, jnp.bfloat16
LOG2E = math.log2(math.e)
HEADS, WIDTH, LEVELS, CELLS = 8, 512, 32, 128
HS = WIDTH // HEADS
X = 40


def dot(a, b):
    return jnp.dot(a, b, preferred_element_type=F32)


def dot_t(a, b):
    return lax.dot_general(a, b, (((1,), (1,)), ((), ())), precision=lax.Precision.HIGHEST, preferred_element_type=F32)


def split3(a):
    hi = a.astype(BF16).astype(F32)
    mid = (a - hi).astype(BF16).astype(F32)
    return hi, mid, a - hi - mid


def spread(a):
    hi, mid, lo = split3(a)
    return (hi + pltpu.roll(mid, X, 1) + pltpu.roll(lo, 2 * X, 1)).astype(BF16)


def prepare_maps(w_in, table, gain_attn, wq, wk, wv, wm, gain_head, w_tend, temper, lk, ls, lf, tcol):
    emb = jnp.concatenate([w_in[...].astype(F32), jnp.zeros((4, WIDTH), F32), table[...]], axis=0)
    xg3 = jnp.concatenate(split3(emb * gain_attn[...]), axis=0).astype(BF16)

    def through(w):
        a = dot(xg3, w[...])
        return a[:X] + a[X : 2 * X] + a[2 * X :]

    aq, ak, av = through(wq), through(wk), through(wv)
    pad = jnp.zeros((128 - X, WIDTH), F32)
    aq_p = jnp.concatenate([aq, pad], axis=0)
    ak_p = jnp.concatenate([ak, pad], axis=0)
    head = lax.broadcasted_iota(jnp.int32, (X, WIDTH), 1) // HS

    def by_head(a):
        return jnp.concatenate([jnp.where(head == h, a, 0.0) for h in range(HEADS)], axis=0)

    kb = by_head(ak)
    qb = by_head(aq)
    s_map = dot_t(kb, aq_p)
    kk = dot_t(kb, ak_p)
    qq = dot_t(qb, aq_p)
    ee = dot_t(emb, jnp.concatenate([emb, pad], axis=0))
    lane = lax.broadcasted_iota(jnp.int32, (1, 128), 1)
    twice = jnp.where(lane < 8, 1.0, 2.0)
    r40 = lax.broadcasted_iota(jnp.int32, (X, 128), 0)
    l40 = lax.broadcasted_iota(jnp.int32, (X, 128), 1)
    diag = (r40 == l40) & (r40 >= 8)

    def norm_rows(g):
        return [g[i : i + 1] * twice for i in range(4)] + [jnp.sum(jnp.where(diag, g, 0.0), axis=0, keepdims=True)]

    def norm_map(gram):
        per = [norm_rows(gram[X * h : X * h + X]) for h in range(HEADS)]
        return jnp.concatenate([per[h][i] for i in range(5) for h in range(HEADS)], axis=0)

    e_rows = norm_rows(ee) + [jnp.zeros((3, 128), F32)]
    lk[...] = spread(jnp.concatenate([norm_map(kk)] + e_rows, axis=0))
    ls[0:320] = spread(s_map)
    ls[320:360] = spread(norm_map(qq))
    ls[360:368] = jnp.zeros((8, 128), BF16)

    vh, vm, _ = split3(by_head(av))
    c = dot(vh.astype(BF16), wm[...]) + dot(vm.astype(BF16), wm[...])
    eh, em, el = split3(emb)
    rows = [c[X * h + 8 : X * h + X] for h in range(HEADS)]
    rows += [jnp.broadcast_to(c[X * h + i : X * h + i + 1], (4, WIDTH)) for h in range(HEADS) for i in range(4)]
    rows += [eh, em, el, jnp.zeros((8, WIDTH), F32)]
    lft = jnp.concatenate(rows, axis=0)
    wt = jnp.concatenate([w_tend[...].astype(F32), jnp.zeros((12, WIDTH), F32)], axis=0) * gain_head[...]
    t = dot_t(wt, lft)
    th = t[:8].astype(BF16).astype(F32)
    lf[0:512] = lft.T.astype(BF16)
    lf[512:528] = jnp.concatenate([th, t[:8] - th], axis=0).astype(BF16)
    square = (HEADS, HEADS)
    on_diag = lax.broadcasted_iota(jnp.int32, square, 0) == lax.broadcasted_iota(jnp.int32, square, 1)
    scale = jnp.sum(jnp.where(on_diag, temper[...], 0.0), axis=1, keepdims=True) * (LOG2E / math.sqrt(HS))
    tcol[...] = jnp.broadcast_to(scale, (HEADS, 128))


def token_rows(fl, l):
    lev = lax.broadcasted_iota(jnp.int32, (LEVELS, CELLS), 0) == l
    one = jnp.concatenate([fl[l], lev.astype(F32)], axis=0)
    return jnp.concatenate([one, one, one, jnp.zeros((8, CELLS), F32)], axis=0).astype(BF16)


def norms_at(out, f, base, epsq, scale):
    n = out[base + 32 : base + 40]
    for i in range(4):
        n = n + f[i : i + 1] * out[base + 8 * i : base + 8 * i + 8]
    return lax.rsqrt(jnp.maximum(n, 0.0) * (1.0 / HS) + epsq) * scale


def key_chunk(base, pairs, fl, lk, rk, rs, eq):
    for l0 in [base + 2 * j for j in range(pairs)]:
        x = jnp.concatenate([token_rows(fl, l0), token_rows(fl, l0 + 1)], axis=1)
        both = dot(lk[...], x)
        for a in range(2):
            l = l0 + a
            out = both[:, 128 * a : 128 * a + 128]
            f = fl[l]
            n = out[44:45]
            for i in range(4):
                n = n + f[i : i + 1] * out[40 + i : 41 + i]
            ms = jnp.maximum(n, 0.0) * (1.0 / WIDTH) + EPS
            rs[pl.ds(l, 1), :] = lax.rsqrt(ms)
            eq[pl.ds(l, 1), :] = EPS * ms
            rk[:, l, :] = norms_at(out, f, 0, EPS * ms, 1.0)


def score_terms(l0, fl, ls):
    x = jnp.concatenate([token_rows(fl, l0), token_rows(fl, l0 + 1)], axis=1)
    return x, dot(ls[...], x)


def attend(l0, x, out, fl, fm, bias, tcol, rk, rs, eq):
    parts = []
    low = lax.broadcasted_iota(jnp.int32, (8, CELLS), 0) < 4
    for a in range(2):
        o = out[:, 128 * a : 128 * a + 128]
        rq = norms_at(o, fl[l0 + a], 320, eq[pl.ds(l0 + a, 1), :], tcol[...])
        probs, sums = [], []
        for h in range(HEADS):
            s = o[X * h + 8 : X * h + X]
            for i in range(4):
                s = s + fm[i] * o[X * h + i : X * h + i + 1]
            s = s * rk[h] * rq[h : h + 1] + bias[...]
            p = jnp.exp2(s - jnp.max(s, axis=0, keepdims=True))
            p = p * (1.0 / jnp.sum(p, axis=0, keepdims=True)) * rs[...]
            probs.append(p)
            z = [p * fm[i] for i in range(4)]
            z = [a[0:8] + a[8:16] + a[16:24] + a[24:32] for a in z]
            for i in (0, 2):
                sums.append(jnp.where(low, z[i], z[i + 1]) + pltpu.roll(jnp.where(low, z[i + 1], z[i]), 4, 0))
        parts.append(jnp.concatenate(probs + sums, axis=0).astype(BF16))
    return jnp.concatenate([jnp.concatenate(parts, axis=1), x], axis=0)


def finish(l0, rhs, lf, ot):
    fin = dot(lf[...], rhs)
    stream = fin[:512]
    ms = jnp.mean(stream * stream, axis=0, keepdims=True)
    tend = (fin[512:520] + fin[520:528]) * lax.rsqrt(ms + EPS)
    ot[l0] = tend[:, :128]
    ot[l0 + 1] = tend[:, 128:]


def query_pairs(levels, fl, fm, bias, ls, lf, tcol, rk, rs, eq, ot, done=lambda n: None):
    pairs = len(levels)
    first, second = {}, {}
    for step in range(pairs + 2):
        if step < pairs:
            first[step] = score_terms(levels[step], fl, ls)
        if step >= 2:
            finish(levels[step - 2], second.pop(step - 2), lf, ot)
            done(step - 2)
        if 1 <= step <= pairs:
            second[step - 1] = attend(levels[step - 1], *first.pop(step - 1), fl, fm, bias, tcol, rk, rs, eq)


ROWS = 4
KL = 8
MESH = pl.DeviceIdType.MESH


NAMES = ("p", "u", "v", "w", "cx", "cy", "cz", "sl", "cp")
EASTWARD = [(n, x) for n in NAMES for x in range(1 if n in ("p", "u", "cx", "sl") else 2, ROWS)]
WESTWARD = [(n, x) for n in NAMES for x in range(3 if n == "p" else 2)]
HALF = KL // 2
ROUTES = [(dx, dk) for dx in (1, -1, 0) for dk in (0, 1, -1) if (dx, dk) != (0, 0)]


def message_rows(dx, dk):
    if dx == 0:
        return len(NAMES) * HALF * ROWS
    slabs = len(EASTWARD if dx > 0 else WESTWARD)
    return -(-slabs * (HALF if dk else KL) // 16) * 16


def substep(n, p, u, v, w, cx, sl, cy, cz, cp):
    up = {x: pltpu.roll(a, 3 * KL - 1, 0) for x, a in p.items()}
    down = {x: pltpu.roll(a, 1, 0) for x, a in p.items()}
    u = {
        x: u[x] - cx[x] * (p[x + 1] - p[x]) - 0.5 * sl[x] * (up[x] - down[x])
        for x in range(n - 3, ROWS + 2 - n)
    }
    new_p, new_v, new_w = {}, {}, {}
    for x in range(n - 2, ROWS + 2 - n):
        c = p[x]
        wx = w[x] - cz[x] * (up[x] - c)
        vx = v[x] - cy[x] * (pltpu.roll(c, CELLS - 1, 1) - c)
        div = (u[x] - u[x - 1]) + (vx - pltpu.roll(vx, 1, 1)) + (wx - pltpu.roll(wx, 1, 0))
        new_p[x] = c - cp[x] * div
        new_v[x] = vx
        new_w[x] = wx
    return new_p, u, new_v, new_w


def whole(tiles, levs, *refs):
    hbm, out, held, in_sem, rest = refs[:17], refs[17], refs[18:35], refs[35], refs[36:]
    (state, coef_x, coef_y, coef_z, slope, compress, ground, temper, w_in, table, gain_attn, gain_head, w_tend,
     wq, wk, wv, wm) = held
    (fl, ot, lk, ls, lf, tcol, rk, rs, eq, bias, fm,
     halo_ss, halo_rs, feat_s, feat_r, feat_ss, feat_rs, tend_s, tend_r, tend_ss, tend_rs, cur) = rest[:22]
    halo_s, halo_r, wide = rest[22:30], rest[30:38], rest[38:46]
    tile, lev = lax.axis_index("tile"), lax.axis_index("lev")
    near = lev + 1 - 2 * lax.rem(lev, 2)
    peers = [near, lax.rem(lev + 2, levs), lax.rem(near + 2, levs)]
    there = [
        (tile + dx >= 0) & (tile + dx < tiles) & (lev + dk >= 0) & (lev + dk < levs) for dx, dk in ROUTES
    ]
    source_there = [there[ROUTES.index((-dx, -dk))] for dx, dk in ROUTES]

    barrier = pltpu.get_barrier_semaphore()
    for (dx, dk), exists in zip(ROUTES, there):
        if dx:
            @pl.when(exists)
            def _():
                pl.semaphore_signal(barrier, inc=1, device_id=(tile + dx, lev + dk), device_id_type=MESH)
    for to in peers:
        pl.semaphore_signal(barrier, inc=1, device_id=(tile, to), device_id_type=MESH)

    loads = [pltpu.make_async_copy(src, dst, in_sem.at[n]) for n, (src, dst) in enumerate(zip(hbm, held))]
    for copy in loads:
        copy.start()
    for copy in loads[:6]:
        copy.wait()
    held_by = dict(zip(NAMES, [(state, f) for f in range(4)] + [(a, 0) for a in (coef_x, coef_y, coef_z, slope, compress)]))

    def slab(name, x, k=0, count=KL):
        ref, f = held_by[name]
        return ref[pl.ds((f * KL + k) * ROWS + x, count, stride=ROWS), :]

    for i, (dx, dk) in enumerate(ROUTES):
        k = HALF if dk > 0 else 0
        if dx == 0:
            pieces = [ref[(f * KL + k) * ROWS : (f * KL + k + HALF) * ROWS, :] for ref, f in held_by.values()]
        else:
            pieces = [slab(n, x, k, HALF if dk else KL) for n, x in (EASTWARD if dx > 0 else WESTWARD)]
        extra = message_rows(dx, dk) - sum(a.shape[0] for a in pieces)
        if extra:
            pieces.append(jnp.zeros((extra, CELLS), F32))
        halo_s[i][...] = jnp.concatenate(pieces, axis=0).astype(BF16)

        @pl.when(jnp.logical_not(source_there[i]))
        def _():
            halo_r[i][...] = jnp.zeros_like(halo_r[i])

    def halo_copy(i):
        dx, dk = ROUTES[i]
        return pltpu.make_async_remote_copy(
            src_ref=halo_s[i], dst_ref=halo_r[i], send_sem=halo_ss.at[i], recv_sem=halo_rs.at[i],
            device_id=(tile + dx, lev + dk), device_id_type=MESH,
        )

    beside = [exists.astype(jnp.int32) for (dx, dk), exists in zip(ROUTES, there) if dx]
    pl.semaphore_wait(barrier, levs - 1 + sum(beside))
    for i, exists in enumerate(there):
        @pl.when(exists)
        def _():
            halo_copy(i).start()

    for copy in loads[6:]:
        copy.wait()
    m_level = lax.broadcasted_iota(jnp.int32, (LEVELS, CELLS), 0)
    bias[...] = jnp.where(m_level >= ground[pl.ds(lev, 1), :], 0.0, -1e30)
    prepare_maps(w_in, table, gain_attn, wq, wk, wv, wm, gain_head, w_tend, temper, lk, ls, lf, tcol)

    for i in range(len(ROUTES)):
        @pl.when(there[i])
        def _():
            halo_copy(i).wait_send()

        @pl.when(source_there[i])
        def _():
            halo_copy(i).wait_recv()

    got = {}
    for i, (dx, dk) in enumerate(ROUTES):
        rows = message_rows(dx, dk)
        wide[i][0:16] = jnp.zeros((16, CELLS), F32)
        wide[i][16 : 16 + rows] = halo_r[i][...].astype(F32)
        wide[i][16 + rows :] = jnp.zeros((16, CELLS), F32)
        got[dx, dk] = wide[i]

    def column(a, name, x):
        if 0 <= x < ROWS:
            mid = slab(name, x)
            at = 16 + HALF * ROWS * a + x
            lo = got[0, 1][pl.ds(at - HALF * ROWS, KL, stride=ROWS), :]
            hi = got[0, -1][pl.ds(at, KL, stride=ROWS), :]
        else:
            dx = 1 if x < 0 else -1
            n = (EASTWARD if x < 0 else WESTWARD).index((name, x + ROWS if x < 0 else x - ROWS))
            mid = got[dx, 0][16 + KL * n : 16 + KL * n + KL, :]
            lo = got[dx, 1][16 + HALF * (n - 1) : 16 + HALF * (n + 1), :]
            hi = got[dx, -1][16 + HALF * n : 16 + HALF * (n + 2), :]
        return jnp.concatenate([lo, mid, hi], axis=0)

    held_x = {n: [x for x in range(-3, 7) if 0 <= x < ROWS or (n, x + ROWS) in EASTWARD and x < 0 or (n, x - ROWS) in WESTWARD and x >= ROWS] for n in NAMES}
    field = {n: {x: column(a, n, x) for x in held_x[n]} for a, n in enumerate(NAMES)}
    p, u, v, w = field["p"], field["u"], field["v"], field["w"]
    for n in range(3):
        p, u, v, w = substep(n, p, u, v, w, *[field[m] for m in ("cx", "sl", "cy", "cz", "cp")])

    mid = slice(KL, 2 * KL)
    for x in range(ROWS):
        fields = jnp.concatenate([a[x][mid] for a in (p, u, v, w)], axis=0)
        cur[x] = fields
        feat_s[x] = fields.astype(BF16)

    def feature_copy(n):
        to = peers[n]
        return pltpu.make_async_remote_copy(
            src_ref=feat_s.at[to], dst_ref=feat_r.at[lev], send_sem=feat_ss.at[n], recv_sem=feat_rs.at[n],
            device_id=(tile, to), device_id_type=MESH,
        )

    for n in (1, 2, 0):
        feature_copy(n).start()
    fl[...] = jnp.zeros_like(fl)

    def take(features, s):
        for f in range(4):
            a = features[KL * f : KL * f + KL].astype(F32)
            at = pl.ds(pl.multiple_of(s * KL, KL), KL)
            fm[f, at] = a
            fl[at, f, :] = a
        key_chunk(s * KL, KL // 2, fl, lk, rk, rs, eq)

    take(feat_s[lev], lev)
    for n, s in enumerate(peers):
        feature_copy(n).wait_recv()
        take(feat_r[s], s)

    def tendency_copy(n):
        to = peers[n]
        return pltpu.make_async_remote_copy(
            src_ref=tend_s.at[to], dst_ref=tend_r.at[lev], send_sem=tend_ss.at[n], recv_sem=tend_rs.at[n],
            device_id=(tile, to), device_id_type=MESH,
        )

    turns = (1, 2, 0)
    blocks = [peers[n] for n in turns] + [lev]

    def done(n):
        d, j = n // (KL // 2), n % (KL // 2)
        if j == KL // 2 - 1:
            to = blocks[d]
            for f in range(4):
                tend_s[to, KL * f : KL * f + KL] = ot[pl.ds(pl.multiple_of(to * KL, KL), KL), f, :]
            if d < levs - 1:
                tendency_copy(turns[d]).start()

    query_pairs(
        [to * KL + k for to in blocks for k in range(0, KL, 2)], fl, fm, bias, ls, lf, tcol, rk, rs, eq, ot, done
    )
    tend_r[lev] = tend_s[lev]
    for n in range(levs - 1):
        feature_copy(n).wait_send()
        tendency_copy(n).wait()
    for x in range(ROWS):
        for f in range(4):
            rows = slice(KL * f, KL * f + KL)
            out[pl.ds(f * KL * ROWS + x, KL, stride=ROWS), :] = cur[x, rows] + tend_r[x, rows]


def shards(state, coef_x, coef_y, coef_z, slope, compress, ground, w_in, level_table, gain_attn,
           w_query, w_key, w_value, w_mix, temper, gain_head, w_tend):
    tiles, levs = lax.axis_size("tile"), lax.axis_size("lev")
    dma = pltpu.SemaphoreType.DMA

    def buf(*shape, dtype=F32):
        return pltpu.VMEM(shape, dtype)

    def pair(*shape):
        return [buf(*shape), buf(*shape)]

    flat = KL * ROWS
    operands = (
        state.reshape(4 * flat, CELLS), *[a.reshape(flat, CELLS) for a in (coef_x, coef_y, coef_z, slope, compress)],
        ground, temper.reshape(1, HEADS), w_in, level_table, gain_attn.reshape(1, WIDTH), gain_head.reshape(1, WIDTH),
        w_tend.T, w_query, w_key, w_value, w_mix,
    )
    result = pl.pallas_call(
        lambda *refs: whole(tiles, levs, *refs),
        out_shape=jax.ShapeDtypeStruct((4 * flat, CELLS), F32),
        in_specs=[pl.BlockSpec(memory_space=pl.ANY)] * len(operands),
        out_specs=pl.BlockSpec(memory_space=pltpu.VMEM),
        scratch_shapes=[
            *[buf(*a.shape, dtype=a.dtype) for a in operands], dma((len(operands),)),
            buf(LEVELS, 8, CELLS), buf(LEVELS, 8, CELLS),
            buf(48, 128, dtype=BF16), buf(368, 128, dtype=BF16), buf(528, 512, dtype=BF16),
            buf(8, 128), buf(HEADS, LEVELS, CELLS), buf(LEVELS, CELLS), buf(LEVELS, CELLS), buf(LEVELS, CELLS),
            buf(4, LEVELS, CELLS),
            dma((len(ROUTES),)), dma((len(ROUTES),)),
            *[buf(levs, 4 * KL, CELLS, dtype=BF16)] * 2, dma((levs - 1,)), dma((levs - 1,)),
            *pair(levs, 4 * KL, CELLS), dma((levs - 1,)), dma((levs - 1,)),
            buf(ROWS, 4 * KL, CELLS),
            *[buf(message_rows(*r), CELLS, dtype=BF16) for r in ROUTES] * 2,
            *[buf(message_rows(*r) + 32, CELLS) for r in ROUTES],
        ],
        compiler_params=pltpu.CompilerParams(
            collective_id=0, has_side_effects=True, vmem_limit_bytes=60 * 2**20
        ),
        name="substeps_and_columns",
    )(*operands)
    return result.reshape(4, KL, ROWS, CELLS)


def solution(mesh):
    block = P("lev", "tile", None)
    placed = (P(None, "lev", "tile", None),) + (block,) * 5 + (P("tile", None),) + (P(),) * 10
    return jax.shard_map(
        shards, mesh=mesh, in_specs=placed, out_specs=P(None, "lev", "tile", None), check_vma=False
    )
```

```python
import math

import jax
import jax.numpy as jnp
from jax import lax
from jax.experimental import pallas as pl
from jax.experimental.pallas import tpu as pltpu
from jax.sharding import PartitionSpec as P

EPS = 1e-6
F32, BF16 = jnp.float32, jnp.bfloat16
LOG2E = math.log2(math.e)
HEADS, WIDTH, LEVELS, CELLS = 8, 512, 32, 128
HS = WIDTH // HEADS
X = 40


def dot(a, b):
    return jnp.dot(a, b, preferred_element_type=F32)


def dot_t(a, b):
    return lax.dot_general(a, b, (((1,), (1,)), ((), ())), precision=lax.Precision.HIGHEST, preferred_element_type=F32)


def split3(a):
    hi = a.astype(BF16).astype(F32)
    mid = (a - hi).astype(BF16).astype(F32)
    return hi, mid, a - hi - mid


def spread(a):
    hi, mid, lo = split3(a)
    return (hi + pltpu.roll(mid, X, 1) + pltpu.roll(lo, 2 * X, 1)).astype(BF16)


def prepare_maps(w_in, table, gain_attn, wq, wk, wv, wm, gain_head, w_tend, temper, lk, ls, lf, tcol):
    emb = jnp.concatenate([w_in[...].astype(F32), jnp.zeros((4, WIDTH), F32), table[...]], axis=0)
    xg3 = jnp.concatenate(split3(emb * gain_attn[...]), axis=0).astype(BF16)

    def through(w):
        a = dot(xg3, w[...])
        return a[:X] + a[X : 2 * X] + a[2 * X :]

    aq, ak, av = through(wq), through(wk), through(wv)
    pad = jnp.zeros((128 - X, WIDTH), F32)
    aq_p = jnp.concatenate([aq, pad], axis=0)
    ak_p = jnp.concatenate([ak, pad], axis=0)
    head = lax.broadcasted_iota(jnp.int32, (X, WIDTH), 1) // HS

    def by_head(a):
        return jnp.concatenate([jnp.where(head == h, a, 0.0) for h in range(HEADS)], axis=0)

    kb = by_head(ak)
    qb = by_head(aq)
    s_map = dot_t(kb, aq_p)
    kk = dot_t(kb, ak_p)
    qq = dot_t(qb, aq_p)
    ee = dot_t(emb, jnp.concatenate([emb, pad], axis=0))
    lane = lax.broadcasted_iota(jnp.int32, (1, 128), 1)
    twice = jnp.where(lane < 8, 1.0, 2.0)
    r40 = lax.broadcasted_iota(jnp.int32, (X, 128), 0)
    l40 = lax.broadcasted_iota(jnp.int32, (X, 128), 1)
    diag = (r40 == l40) & (r40 >= 8)

    def norm_rows(g):
        return [g[i : i + 1] * twice for i in range(4)] + [jnp.sum(jnp.where(diag, g, 0.0), axis=0, keepdims=True)]

    def norm_map(gram):
        per = [norm_rows(gram[X * h : X * h + X]) for h in range(HEADS)]
        return jnp.concatenate([per[h][i] for i in range(5) for h in range(HEADS)], axis=0)

    e_rows = norm_rows(ee) + [jnp.zeros((3, 128), F32)]
    lk[...] = spread(jnp.concatenate([norm_map(kk)] + e_rows, axis=0))
    ls[0:320] = spread(s_map)
    ls[320:360] = spread(norm_map(qq))
    ls[360:368] = jnp.zeros((8, 128), BF16)

    vh, vm, _ = split3(by_head(av))
    c = dot(vh.astype(BF16), wm[...]) + dot(vm.astype(BF16), wm[...])
    eh, em, el = split3(emb)
    rows = [c[X * h + 8 : X * h + X] for h in range(HEADS)]
    rows += [jnp.broadcast_to(c[X * h + i : X * h + i + 1], (4, WIDTH)) for h in range(HEADS) for i in range(4)]
    rows += [eh, em, el, jnp.zeros((8, WIDTH), F32)]
    lft = jnp.concatenate(rows, axis=0)
    wt = jnp.concatenate([w_tend[...].astype(F32), jnp.zeros((12, WIDTH), F32)], axis=0) * gain_head[...]
    t = dot_t(wt, lft)
    th = t[:8].astype(BF16).astype(F32)
    lf[0:512] = lft.T.astype(BF16)
    lf[512:528] = jnp.concatenate([th, t[:8] - th], axis=0).astype(BF16)
    square = (HEADS, HEADS)
    on_diag = lax.broadcasted_iota(jnp.int32, square, 0) == lax.broadcasted_iota(jnp.int32, square, 1)
    scale = jnp.sum(jnp.where(on_diag, temper[...], 0.0), axis=1, keepdims=True) * (LOG2E / math.sqrt(HS))
    tcol[...] = jnp.broadcast_to(scale, (HEADS, 128))


def token_rows(fl, l):
    lev = lax.broadcasted_iota(jnp.int32, (LEVELS, CELLS), 0) == l
    one = jnp.concatenate([fl[l], lev.astype(F32)], axis=0)
    return jnp.concatenate([one, one, one, jnp.zeros((8, CELLS), F32)], axis=0).astype(BF16)


def norms_at(out, f, base, epsq, scale):
    n = out[base + 32 : base + 40]
    for i in range(4):
        n = n + f[i : i + 1] * out[base + 8 * i : base + 8 * i + 8]
    return lax.rsqrt(jnp.maximum(n, 0.0) * (1.0 / HS) + epsq) * scale


def key_chunk(base, pairs, fl, lk, rk, rs, eq):
    for l0 in [base + 2 * j for j in range(pairs)]:
        x = jnp.concatenate([token_rows(fl, l0), token_rows(fl, l0 + 1)], axis=1)
        both = dot(lk[...], x)
        for a in range(2):
            l = l0 + a
            out = both[:, 128 * a : 128 * a + 128]
            f = fl[l]
            n = out[44:45]
            for i in range(4):
                n = n + f[i : i + 1] * out[40 + i : 41 + i]
            ms = jnp.maximum(n, 0.0) * (1.0 / WIDTH) + EPS
            rs[pl.ds(l, 1), :] = lax.rsqrt(ms)
            eq[pl.ds(l, 1), :] = EPS * ms
            rk[:, l, :] = norms_at(out, f, 0, EPS * ms, 1.0)


def score_terms(l0, fl, ls):
    x = jnp.concatenate([token_rows(fl, l0), token_rows(fl, l0 + 1)], axis=1)
    return x, dot(ls[...], x)


def attend(l0, x, out, fl, fm, bias, tcol, rk, rs, eq):
    parts = []
    low = lax.broadcasted_iota(jnp.int32, (8, CELLS), 0) < 4
    for a in range(2):
        o = out[:, 128 * a : 128 * a + 128]
        rq = norms_at(o, fl[l0 + a], 320, eq[pl.ds(l0 + a, 1), :], tcol[...])
        probs, sums = [], []
        for h in range(HEADS):
            s = o[X * h + 8 : X * h + X]
            for i in range(4):
                s = s + fm[i] * o[X * h + i : X * h + i + 1]
            s = s * rk[h] * rq[h : h + 1] + bias[...]
            p = jnp.exp2(s - jnp.max(s, axis=0, keepdims=True))
            p = p * (1.0 / jnp.sum(p, axis=0, keepdims=True)) * rs[...]
            probs.append(p)
            z = [p * fm[i] for i in range(4)]
            z = [a[0:8] + a[8:16] + a[16:24] + a[24:32] for a in z]
            for i in (0, 2):
                sums.append(jnp.where(low, z[i], z[i + 1]) + pltpu.roll(jnp.where(low, z[i + 1], z[i]), 4, 0))
        parts.append(jnp.concatenate(probs + sums, axis=0).astype(BF16))
    return jnp.concatenate([jnp.concatenate(parts, axis=1), x], axis=0)


def finish(l0, rhs, lf, ot):
    fin = dot(lf[...], rhs)
    stream = fin[:512]
    ms = jnp.mean(stream * stream, axis=0, keepdims=True)
    tend = (fin[512:520] + fin[520:528]) * lax.rsqrt(ms + EPS)
    ot[l0] = tend[:, :128]
    ot[l0 + 1] = tend[:, 128:]


def query_pairs(levels, fl, fm, bias, ls, lf, tcol, rk, rs, eq, ot, done=lambda n: None):
    pairs = len(levels)
    first, second = {}, {}
    for step in range(pairs + 2):
        if step < pairs:
            first[step] = score_terms(levels[step], fl, ls)
        if step >= 2:
            finish(levels[step - 2], second.pop(step - 2), lf, ot)
            done(step - 2)
        if 1 <= step <= pairs:
            second[step - 1] = attend(levels[step - 1], *first.pop(step - 1), fl, fm, bias, tcol, rk, rs, eq)


ROWS = 4
KL = 8
MESH = pl.DeviceIdType.MESH


NAMES = ("p", "u", "v", "w", "cx", "cy", "cz", "sl", "cp")
EASTWARD = [(n, x) for n in NAMES for x in range(1 if n in ("p", "u", "cx", "sl") else 2, ROWS)]
WESTWARD = [(n, x) for n in NAMES for x in range(3 if n == "p" else 2)]
ROUTES = [(dx, dk) for dx in (1, -1, 0) for dk in (0, 1, -1) if (dx, dk) != (0, 0)]
MARGIN = 32


def slots(dx, dk):
    tall = ("p", "w", "cz")
    if dx == 0:
        wanted = [((n, None), 3 if n in tall else 2) for n in NAMES]
    elif dk == 0:
        wanted = [(s, KL) for s in (EASTWARD if dx > 0 else WESTWARD)]
    elif dx > 0:
        wanted = [(s, 3 if s[0] == "p" or s[0] in tall and dk > 0 else 2) for s in EASTWARD]
    else:
        wanted = [((n, x), 2 - x if n in tall else 1) for n in NAMES for x in range(2 if n in tall else 1)]
    table, row = {}, 0
    for key, levels in wanted:
        table[key] = row, levels
        row += levels * (ROWS if dx == 0 else 1)
    return table, -(-row // 16) * 16


def substep(n, p, u, v, w, cx, sl, cy, cz, cp):
    up = {x: pltpu.roll(a, 3 * KL - 1, 0) for x, a in p.items()}
    down = {x: pltpu.roll(a, 1, 0) for x, a in p.items()}
    u = {
        x: u[x] - cx[x] * (p[x + 1] - p[x]) - 0.5 * sl[x] * (up[x] - down[x])
        for x in range(n - 3, ROWS + 2 - n)
    }
    new_p, new_v, new_w = {}, {}, {}
    for x in range(n - 2, ROWS + 2 - n):
        c = p[x]
        wx = w[x] - cz[x] * (up[x] - c)
        vx = v[x] - cy[x] * (pltpu.roll(c, CELLS - 1, 1) - c)
        div = (u[x] - u[x - 1]) + (vx - pltpu.roll(vx, 1, 1)) + (wx - pltpu.roll(wx, 1, 0))
        new_p[x] = c - cp[x] * div
        new_v[x] = vx
        new_w[x] = wx
    return new_p, u, new_v, new_w


def whole(tiles, levs, *refs):
    hbm, out, held, in_sem, rest = refs[:17], refs[17], refs[18:35], refs[35], refs[36:]
    (state, coef_x, coef_y, coef_z, slope, compress, ground, temper, w_in, table, gain_attn, gain_head, w_tend,
     wq, wk, wv, wm) = held
    (fl, ot, lk, ls, lf, tcol, rk, rs, eq, bias, fm,
     halo_ss, halo_rs, feat_s, feat_r, feat_ss, feat_rs, tend_s, tend_r, tend_ss, tend_rs, cur) = rest[:22]
    halo_s, halo_r, wide = rest[22:30], rest[30:38], rest[38:46]
    tile, lev = lax.axis_index("tile"), lax.axis_index("lev")
    near = lev + 1 - 2 * lax.rem(lev, 2)
    peers = [near, lax.rem(lev + 2, levs), lax.rem(near + 2, levs)]
    there = [
        (tile + dx >= 0) & (tile + dx < tiles) & (lev + dk >= 0) & (lev + dk < levs) for dx, dk in ROUTES
    ]
    source_there = [there[ROUTES.index((-dx, -dk))] for dx, dk in ROUTES]

    barrier = pltpu.get_barrier_semaphore()
    for (dx, dk), exists in zip(ROUTES, there):
        if dx:
            @pl.when(exists)
            def _():
                pl.semaphore_signal(barrier, inc=1, device_id=(tile + dx, lev + dk), device_id_type=MESH)
    for to in peers:
        pl.semaphore_signal(barrier, inc=1, device_id=(tile, to), device_id_type=MESH)

    loads = [pltpu.make_async_copy(src, dst, in_sem.at[n]) for n, (src, dst) in enumerate(zip(hbm, held))]
    for copy in loads:
        copy.start()
    for copy in loads[:6]:
        copy.wait()
    held_by = dict(zip(NAMES, [(state, f) for f in range(4)] + [(a, 0) for a in (coef_x, coef_y, coef_z, slope, compress)]))

    def slab(name, x, k=0, count=KL):
        ref, f = held_by[name]
        return ref[pl.ds((f * KL + k) * ROWS + x, count, stride=ROWS), :]

    for i, (dx, dk) in enumerate(ROUTES):
        layout, rows = slots(dx, dk)
        pieces = []
        for (name, x), (_, levels) in layout.items():
            k = KL - levels if dk > 0 else 0
            if dx == 0:
                ref, f = held_by[name]
                pieces.append(ref[(f * KL + k) * ROWS : (f * KL + k + levels) * ROWS, :])
            else:
                pieces.append(slab(name, x, k, levels))
        extra = rows - sum(a.shape[0] for a in pieces)
        if extra:
            pieces.append(jnp.zeros((extra, CELLS), F32))
        halo_s[i][...] = jnp.concatenate(pieces, axis=0).astype(BF16)

        @pl.when(jnp.logical_not(source_there[i]))
        def _():
            halo_r[i][...] = jnp.zeros_like(halo_r[i])

    def halo_copy(i):
        dx, dk = ROUTES[i]
        return pltpu.make_async_remote_copy(
            src_ref=halo_s[i], dst_ref=halo_r[i], send_sem=halo_ss.at[i], recv_sem=halo_rs.at[i],
            device_id=(tile + dx, lev + dk), device_id_type=MESH,
        )

    beside = [exists.astype(jnp.int32) for (dx, dk), exists in zip(ROUTES, there) if dx]
    pl.semaphore_wait(barrier, levs - 1 + sum(beside))
    for i, exists in enumerate(there):
        @pl.when(exists)
        def _():
            halo_copy(i).start()

    for copy in loads[6:]:
        copy.wait()
    m_level = lax.broadcasted_iota(jnp.int32, (LEVELS, CELLS), 0)
    bias[...] = jnp.where(m_level >= ground[pl.ds(lev, 1), :], 0.0, -1e30)
    prepare_maps(w_in, table, gain_attn, wq, wk, wv, wm, gain_head, w_tend, temper, lk, ls, lf, tcol)

    for i in range(len(ROUTES)):
        @pl.when(there[i])
        def _():
            halo_copy(i).wait_send()

        @pl.when(source_there[i])
        def _():
            halo_copy(i).wait_recv()

    got = {}
    for i, (dx, dk) in enumerate(ROUTES):
        rows = slots(dx, dk)[1]
        wide[i][0:MARGIN] = jnp.zeros((MARGIN, CELLS), F32)
        wide[i][MARGIN : MARGIN + rows] = halo_r[i][...].astype(F32)
        wide[i][MARGIN + rows :] = jnp.zeros((MARGIN, CELLS), F32)
        got[dx, dk] = wide[i]

    def column(name, x):
        dx = 1 if x < 0 else -1 if x >= ROWS else 0
        key = (name, x + ROWS * dx if dx else None)
        parts = []
        for dk in (1, 0, -1):
            if dx == 0 and dk == 0:
                parts.append(slab(name, x))
                continue
            first, levels = slots(dx, dk)[0].get(key, (None, 0))
            if levels == 0:
                parts.append(jnp.zeros((KL, CELLS), F32))
                continue
            stride = 1 if dx else ROWS
            at = MARGIN + first - (stride * (KL - levels) if dk > 0 else 0) + (0 if dx else x)
            parts.append(got[dx, dk][pl.ds(at, KL, stride=stride) if stride > 1 else slice(at, at + KL), :])
        return jnp.concatenate(parts, axis=0)

    held_x = {n: [x for x in range(-3, 7) if 0 <= x < ROWS or (n, x + ROWS) in EASTWARD and x < 0 or (n, x - ROWS) in WESTWARD and x >= ROWS] for n in NAMES}
    field = {n: {x: column(n, x) for x in held_x[n]} for n in NAMES}
    p, u, v, w = field["p"], field["u"], field["v"], field["w"]
    for n in range(3):
        p, u, v, w = substep(n, p, u, v, w, *[field[m] for m in ("cx", "sl", "cy", "cz", "cp")])

    mid = slice(KL, 2 * KL)
    for x in range(ROWS):
        fields = jnp.concatenate([a[x][mid] for a in (p, u, v, w)], axis=0)
        cur[x] = fields
        feat_s[x] = fields.astype(BF16)

    def feature_copy(n):
        to = peers[n]
        return pltpu.make_async_remote_copy(
            src_ref=feat_s.at[to], dst_ref=feat_r.at[lev], send_sem=feat_ss.at[n], recv_sem=feat_rs.at[n],
            device_id=(tile, to), device_id_type=MESH,
        )

    for n in (1, 2, 0):
        feature_copy(n).start()
    fl[...] = jnp.zeros_like(fl)

    def take(features, s):
        for f in range(4):
            a = features[KL * f : KL * f + KL].astype(F32)
            at = pl.ds(pl.multiple_of(s * KL, KL), KL)
            fm[f, at] = a
            fl[at, f, :] = a
        key_chunk(s * KL, KL // 2, fl, lk, rk, rs, eq)

    take(feat_s[lev], lev)
    for n, s in enumerate(peers):
        feature_copy(n).wait_recv()
        take(feat_r[s], s)

    def tendency_copy(n):
        to = peers[n]
        return pltpu.make_async_remote_copy(
            src_ref=tend_s.at[to], dst_ref=tend_r.at[lev], send_sem=tend_ss.at[n], recv_sem=tend_rs.at[n],
            device_id=(tile, to), device_id_type=MESH,
        )

    turns = (1, 2, 0)
    blocks = [peers[n] for n in turns] + [lev]

    def done(n):
        d, j = n // (KL // 2), n % (KL // 2)
        if j == KL // 2 - 1:
            to = blocks[d]
            for f in range(4):
                tend_s[to, KL * f : KL * f + KL] = ot[pl.ds(pl.multiple_of(to * KL, KL), KL), f, :]
            if d < levs - 1:
                tendency_copy(turns[d]).start()

    query_pairs(
        [to * KL + k for to in blocks for k in range(0, KL, 2)], fl, fm, bias, ls, lf, tcol, rk, rs, eq, ot, done
    )
    tend_r[lev] = tend_s[lev]
    for n in range(levs - 1):
        feature_copy(n).wait_send()
        tendency_copy(n).wait()
    for x in range(ROWS):
        for f in range(4):
            rows = slice(KL * f, KL * f + KL)
            out[pl.ds(f * KL * ROWS + x, KL, stride=ROWS), :] = cur[x, rows] + tend_r[x, rows]


def shards(state, coef_x, coef_y, coef_z, slope, compress, ground, w_in, level_table, gain_attn,
           w_query, w_key, w_value, w_mix, temper, gain_head, w_tend):
    tiles, levs = lax.axis_size("tile"), lax.axis_size("lev")
    dma = pltpu.SemaphoreType.DMA

    def buf(*shape, dtype=F32):
        return pltpu.VMEM(shape, dtype)

    def pair(*shape):
        return [buf(*shape), buf(*shape)]

    flat = KL * ROWS
    operands = (
        state.reshape(4 * flat, CELLS), *[a.reshape(flat, CELLS) for a in (coef_x, coef_y, coef_z, slope, compress)],
        ground, temper.reshape(1, HEADS), w_in, level_table, gain_attn.reshape(1, WIDTH), gain_head.reshape(1, WIDTH),
        w_tend.T, w_query, w_key, w_value, w_mix,
    )
    result = pl.pallas_call(
        lambda *refs: whole(tiles, levs, *refs),
        out_shape=jax.ShapeDtypeStruct((4 * flat, CELLS), F32),
        in_specs=[pl.BlockSpec(memory_space=pl.ANY)] * len(operands),
        out_specs=pl.BlockSpec(memory_space=pltpu.VMEM),
        scratch_shapes=[
            *[buf(*a.shape, dtype=a.dtype) for a in operands], dma((len(operands),)),
            buf(LEVELS, 8, CELLS), buf(LEVELS, 8, CELLS),
            buf(48, 128, dtype=BF16), buf(368, 128, dtype=BF16), buf(528, 512, dtype=BF16),
            buf(8, 128), buf(HEADS, LEVELS, CELLS), buf(LEVELS, CELLS), buf(LEVELS, CELLS), buf(LEVELS, CELLS),
            buf(4, LEVELS, CELLS),
            dma((len(ROUTES),)), dma((len(ROUTES),)),
            *[buf(levs, 4 * KL, CELLS, dtype=BF16)] * 2, dma((levs - 1,)), dma((levs - 1,)),
            *pair(levs, 4 * KL, CELLS), dma((levs - 1,)), dma((levs - 1,)),
            buf(ROWS, 4 * KL, CELLS),
            *[buf(slots(*r)[1], CELLS, dtype=BF16) for r in ROUTES] * 2,
            *[buf(slots(*r)[1] + 2 * MARGIN, CELLS) for r in ROUTES],
        ],
        compiler_params=pltpu.CompilerParams(
            collective_id=0, has_side_effects=True, vmem_limit_bytes=60 * 2**20
        ),
        name="substeps_and_columns",
    )(*operands)
    return result.reshape(4, KL, ROWS, CELLS)


def solution(mesh):
    block = P("lev", "tile", None)
    placed = (P(None, "lev", "tile", None),) + (block,) * 5 + (P("tile", None),) + (P(),) * 10
    return jax.shard_map(
        shards, mesh=mesh, in_specs=placed, out_specs=P(None, "lev", "tile", None), check_vma=False
    )
```

```python
import math

import jax
import jax.numpy as jnp
from jax import lax
from jax.experimental import pallas as pl
from jax.experimental.pallas import tpu as pltpu
from jax.sharding import PartitionSpec as P

EPS = 1e-6
F32, BF16 = jnp.float32, jnp.bfloat16
LOG2E = math.log2(math.e)
HEADS, WIDTH, LEVELS, CELLS = 8, 512, 32, 128
HS = WIDTH // HEADS
X = 40


def dot(a, b):
    return jnp.dot(a, b, preferred_element_type=F32)


def dot_t(a, b):
    return lax.dot_general(a, b, (((1,), (1,)), ((), ())), precision=lax.Precision.HIGHEST, preferred_element_type=F32)


def split3(a):
    hi = a.astype(BF16).astype(F32)
    mid = (a - hi).astype(BF16).astype(F32)
    return hi, mid, a - hi - mid


def spread(a):
    hi, mid, lo = split3(a)
    return (hi + pltpu.roll(mid, X, 1) + pltpu.roll(lo, 2 * X, 1)).astype(BF16)


def prepare_maps(w_in, table, gain_attn, wq, wk, wv, wm, gain_head, w_tend, temper, lk, ls, lf, tcol):
    emb = jnp.concatenate([w_in[...].astype(F32), jnp.zeros((4, WIDTH), F32), table[...]], axis=0)
    xg3 = jnp.concatenate(split3(emb * gain_attn[...]), axis=0).astype(BF16)

    def through(w):
        a = dot(xg3, w[...])
        return a[:X] + a[X : 2 * X] + a[2 * X :]

    aq, ak, av = through(wq), through(wk), through(wv)
    pad = jnp.zeros((128 - X, WIDTH), F32)
    aq_p = jnp.concatenate([aq, pad], axis=0)
    ak_p = jnp.concatenate([ak, pad], axis=0)
    head = lax.broadcasted_iota(jnp.int32, (X, WIDTH), 1) // HS

    def by_head(a):
        return jnp.concatenate([jnp.where(head == h, a, 0.0) for h in range(HEADS)], axis=0)

    kb = by_head(ak)
    qb = by_head(aq)
    s_map = dot_t(kb, aq_p)
    kk = dot_t(kb, ak_p)
    qq = dot_t(qb, aq_p)
    ee = dot_t(emb, jnp.concatenate([emb, pad], axis=0))
    lane = lax.broadcasted_iota(jnp.int32, (1, 128), 1)
    twice = jnp.where(lane < 8, 1.0, 2.0)
    r40 = lax.broadcasted_iota(jnp.int32, (X, 128), 0)
    l40 = lax.broadcasted_iota(jnp.int32, (X, 128), 1)
    diag = (r40 == l40) & (r40 >= 8)

    def norm_rows(g):
        return [g[i : i + 1] * twice for i in range(4)] + [jnp.sum(jnp.where(diag, g, 0.0), axis=0, keepdims=True)]

    def norm_map(gram):
        per = [norm_rows(gram[X * h : X * h + X]) for h in range(HEADS)]
        return jnp.concatenate([per[h][i] for i in range(5) for h in range(HEADS)], axis=0)

    e_rows = norm_rows(ee) + [jnp.zeros((3, 128), F32)]
    lk[...] = spread(jnp.concatenate([norm_map(kk)] + e_rows, axis=0))
    ls[0:320] = spread(s_map)
    ls[320:360] = spread(norm_map(qq))
    ls[360:368] = jnp.zeros((8, 128), BF16)

    vh, vm, _ = split3(by_head(av))
    c = dot(vh.astype(BF16), wm[...]) + dot(vm.astype(BF16), wm[...])
    eh, em, el = split3(emb)
    rows = [c[X * h + 8 : X * h + X] for h in range(HEADS)]
    rows += [jnp.broadcast_to(c[X * h + i : X * h + i + 1], (4, WIDTH)) for h in range(HEADS) for i in range(4)]
    rows += [eh, em, el, jnp.zeros((8, WIDTH), F32)]
    lft = jnp.concatenate(rows, axis=0)
    wt = jnp.concatenate([w_tend[...].astype(F32), jnp.zeros((12, WIDTH), F32)], axis=0) * gain_head[...]
    t = dot_t(wt, lft)
    th = t[:8].astype(BF16).astype(F32)
    lf[0:512] = lft.T.astype(BF16)
    lf[512:528] = jnp.concatenate([th, t[:8] - th], axis=0).astype(BF16)
    square = (HEADS, HEADS)
    on_diag = lax.broadcasted_iota(jnp.int32, square, 0) == lax.broadcasted_iota(jnp.int32, square, 1)
    scale = jnp.sum(jnp.where(on_diag, temper[...], 0.0), axis=1, keepdims=True) * (LOG2E / math.sqrt(HS))
    tcol[...] = jnp.broadcast_to(scale, (HEADS, 128))


def token_rows(fl, l):
    lev = lax.broadcasted_iota(jnp.int32, (LEVELS, CELLS), 0) == l
    one = jnp.concatenate([fl[l], lev.astype(F32)], axis=0)
    return jnp.concatenate([one, one, one, jnp.zeros((8, CELLS), F32)], axis=0).astype(BF16)


def norms_at(out, f, base, epsq, scale):
    n = out[base + 32 : base + 40]
    for i in range(4):
        n = n + f[i : i + 1] * out[base + 8 * i : base + 8 * i + 8]
    return lax.rsqrt(jnp.maximum(n, 0.0) * (1.0 / HS) + epsq) * scale


def key_chunk(base, pairs, fl, lk, rk, rs, eq):
    for l0 in [base + 2 * j for j in range(pairs)]:
        x = jnp.concatenate([token_rows(fl, l0), token_rows(fl, l0 + 1)], axis=1)
        both = dot(lk[...], x)
        for a in range(2):
            l = l0 + a
            out = both[:, 128 * a : 128 * a + 128]
            f = fl[l]
            n = out[44:45]
            for i in range(4):
                n = n + f[i : i + 1] * out[40 + i : 41 + i]
            ms = jnp.maximum(n, 0.0) * (1.0 / WIDTH) + EPS
            rs[pl.ds(l, 1), :] = lax.rsqrt(ms)
            eq[pl.ds(l, 1), :] = EPS * ms
            rk[:, l, :] = norms_at(out, f, 0, EPS * ms, 1.0)


def score_terms(l0, fl, ls):
    x = jnp.concatenate([token_rows(fl, l0), token_rows(fl, l0 + 1)], axis=1)
    return x, dot(ls[...], x)


def attend(l0, x, out, fl, fm, bias, tcol, rk, rs, eq):
    parts = []
    low = lax.broadcasted_iota(jnp.int32, (8, CELLS), 0) < 4
    for a in range(2):
        o = out[:, 128 * a : 128 * a + 128]
        rq = norms_at(o, fl[l0 + a], 320, eq[pl.ds(l0 + a, 1), :], tcol[...])
        probs, sums = [], []
        for h in range(HEADS):
            s = o[X * h + 8 : X * h + X]
            for i in range(4):
                s = s + fm[i] * o[X * h + i : X * h + i + 1]
            s = s * rk[h] * rq[h : h + 1] + bias[...]
            p = jnp.exp2(s - jnp.max(s, axis=0, keepdims=True))
            p = p * (1.0 / jnp.sum(p, axis=0, keepdims=True)) * rs[...]
            probs.append(p)
            z = [p * fm[i] for i in range(4)]
            z = [a[0:8] + a[8:16] + a[16:24] + a[24:32] for a in z]
            for i in (0, 2):
                sums.append(jnp.where(low, z[i], z[i + 1]) + pltpu.roll(jnp.where(low, z[i + 1], z[i]), 4, 0))
        parts.append(jnp.concatenate(probs + sums, axis=0).astype(BF16))
    return jnp.concatenate([jnp.concatenate(parts, axis=1), x], axis=0)


def finish(l0, rhs, lf, ot):
    fin = dot(lf[...], rhs)
    stream = fin[:512]
    ms = jnp.mean(stream * stream, axis=0, keepdims=True)
    tend = (fin[512:520] + fin[520:528]) * lax.rsqrt(ms + EPS)
    ot[l0] = tend[:, :128]
    ot[l0 + 1] = tend[:, 128:]


def query_pairs(levels, fl, fm, bias, ls, lf, tcol, rk, rs, eq, ot, done=lambda n: None):
    pairs = len(levels)
    first, second = {}, {}
    for step in range(pairs + 2):
        if step < pairs:
            first[step] = score_terms(levels[step], fl, ls)
        if step >= 2:
            finish(levels[step - 2], second.pop(step - 2), lf, ot)
            done(step - 2)
        if 1 <= step <= pairs:
            second[step - 1] = attend(levels[step - 1], *first.pop(step - 1), fl, fm, bias, tcol, rk, rs, eq)


ROWS = 4
KL = 8
MESH = pl.DeviceIdType.MESH


NAMES = ("p", "u", "v", "w", "cx", "cy", "cz", "sl", "cp")
EASTWARD = [(n, x) for n in NAMES for x in range(1 if n in ("p", "u", "cx", "sl") else 2, ROWS)]
WESTWARD = [(n, x) for n in NAMES for x in range(3 if n == "p" else 2)]
ROUTES = [(dx, dk) for dx in (1, -1, 0) for dk in (0, 1, -1) if (dx, dk) != (0, 0)]
MARGIN = 32


def slots(dx, dk):
    tall = ("p", "w", "cz")
    if dx == 0:
        wanted = [((n, None), 3 if n in tall else 2) for n in NAMES]
    elif dk == 0:
        wanted = [(s, KL) for s in (EASTWARD if dx > 0 else WESTWARD)]
    elif dx > 0:
        wanted = [(s, 3 if s[0] == "p" or s[0] in tall and dk > 0 else 2) for s in EASTWARD]
    else:
        wanted = [((n, x), 2 - x if n in tall else 1) for n in NAMES for x in range(2 if n in tall else 1)]
    table, row = {}, 0
    for key, levels in wanted:
        table[key] = row, levels
        row += levels * (ROWS if dx == 0 else 1)
    return table, -(-row // 16) * 16


def substep(n, p, u, v, w, cx, sl, cy, cz, cp):
    up = {x: pltpu.roll(a, 3 * KL - 1, 0) for x, a in p.items()}
    down = {x: pltpu.roll(a, 1, 0) for x, a in p.items()}
    u = {
        x: u[x] - cx[x] * (p[x + 1] - p[x]) - 0.5 * sl[x] * (up[x] - down[x])
        for x in range(n - 3, ROWS + 2 - n)
    }
    new_p, new_v, new_w = {}, {}, {}
    for x in range(n - 2, ROWS + 2 - n):
        c = p[x]
        wx = w[x] - cz[x] * (up[x] - c)
        vx = v[x] - cy[x] * (pltpu.roll(c, CELLS - 1, 1) - c)
        div = (u[x] - u[x - 1]) + (vx - pltpu.roll(vx, 1, 1)) + (wx - pltpu.roll(wx, 1, 0))
        new_p[x] = c - cp[x] * div
        new_v[x] = vx
        new_w[x] = wx
    return new_p, u, new_v, new_w


def whole(tiles, levs, *refs):
    hbm, out, held, in_sem, rest = refs[:17], refs[17], refs[18:35], refs[35], refs[36:]
    (state, coef_x, coef_y, coef_z, slope, compress, ground, temper, w_in, table, gain_attn, gain_head, w_tend,
     wq, wk, wv, wm) = held
    (fl, ot, lk, ls, lf, tcol, rk, rs, eq, bias, fm,
     halo_ss, halo_rs, feat_s, feat_r, feat_ss, feat_rs, tend_s, tend_r, tend_ss, tend_rs, cur) = rest[:22]
    halo_s, halo_r, wide = rest[22:30], rest[30:38], rest[38:46]
    tile, lev = lax.axis_index("tile"), lax.axis_index("lev")
    near = lev + 1 - 2 * lax.rem(lev, 2)
    peers = [near, lax.rem(lev + 2, levs), lax.rem(near + 2, levs)]
    there = [
        (tile + dx >= 0) & (tile + dx < tiles) & (lev + dk >= 0) & (lev + dk < levs) for dx, dk in ROUTES
    ]
    source_there = [there[ROUTES.index((-dx, -dk))] for dx, dk in ROUTES]

    barrier = pltpu.get_barrier_semaphore()
    for (dx, dk), exists in zip(ROUTES, there):
        if dx:
            @pl.when(exists)
            def _():
                pl.semaphore_signal(barrier, inc=1, device_id=(tile + dx, lev + dk), device_id_type=MESH)
    for to in peers:
        pl.semaphore_signal(barrier, inc=1, device_id=(tile, to), device_id_type=MESH)

    loads = [pltpu.make_async_copy(src, dst, in_sem.at[n]) for n, (src, dst) in enumerate(zip(hbm, held))]
    for copy in loads:
        copy.start()
    for copy in loads[:6]:
        copy.wait()
    held_by = dict(zip(NAMES, [(state, f) for f in range(4)] + [(a, 0) for a in (coef_x, coef_y, coef_z, slope, compress)]))

    def slab(name, x, k=0, count=KL):
        ref, f = held_by[name]
        return ref[pl.ds((f * KL + k) * ROWS + x, count, stride=ROWS), :]

    for i, (dx, dk) in enumerate(ROUTES):
        layout, rows = slots(dx, dk)
        pieces = []
        for (name, x), (_, levels) in layout.items():
            k = KL - levels if dk > 0 else 0
            if dx == 0:
                ref, f = held_by[name]
                pieces.append(ref[(f * KL + k) * ROWS : (f * KL + k + levels) * ROWS, :])
            else:
                pieces.append(slab(name, x, k, levels))
        extra = rows - sum(a.shape[0] for a in pieces)
        if extra:
            pieces.append(jnp.zeros((extra, CELLS), F32))
        halo_s[i][...] = jnp.concatenate(pieces, axis=0).astype(BF16)

        @pl.when(jnp.logical_not(source_there[i]))
        def _():
            halo_r[i][...] = jnp.zeros_like(halo_r[i])

    def halo_copy(i):
        dx, dk = ROUTES[i]
        return pltpu.make_async_remote_copy(
            src_ref=halo_s[i], dst_ref=halo_r[i], send_sem=halo_ss.at[i], recv_sem=halo_rs.at[i],
            device_id=(tile + dx, lev + dk), device_id_type=MESH,
        )

    beside = [exists.astype(jnp.int32) for (dx, dk), exists in zip(ROUTES, there) if dx]
    pl.semaphore_wait(barrier, levs - 1 + sum(beside))
    for i in (1, 2, 0, 4, 5, 3, 6, 7):
        @pl.when(there[i])
        def _():
            halo_copy(i).start()

    for copy in loads[6:]:
        copy.wait()
    m_level = lax.broadcasted_iota(jnp.int32, (LEVELS, CELLS), 0)
    bias[...] = jnp.where(m_level >= ground[pl.ds(lev, 1), :], 0.0, -1e30)
    prepare_maps(w_in, table, gain_attn, wq, wk, wv, wm, gain_head, w_tend, temper, lk, ls, lf, tcol)

    for i in range(len(ROUTES)):
        @pl.when(there[i])
        def _():
            halo_copy(i).wait_send()

        @pl.when(source_there[i])
        def _():
            halo_copy(i).wait_recv()

    got = {}
    for i, (dx, dk) in enumerate(ROUTES):
        rows = slots(dx, dk)[1]
        wide[i][0:MARGIN] = jnp.zeros((MARGIN, CELLS), F32)
        wide[i][MARGIN : MARGIN + rows] = halo_r[i][...].astype(F32)
        wide[i][MARGIN + rows :] = jnp.zeros((MARGIN, CELLS), F32)
        got[dx, dk] = wide[i]

    def column(name, x):
        dx = 1 if x < 0 else -1 if x >= ROWS else 0
        key = (name, x + ROWS * dx if dx else None)
        parts = []
        for dk in (1, 0, -1):
            if dx == 0 and dk == 0:
                parts.append(slab(name, x))
                continue
            first, levels = slots(dx, dk)[0].get(key, (None, 0))
            if levels == 0:
                parts.append(jnp.zeros((KL, CELLS), F32))
                continue
            stride = 1 if dx else ROWS
            at = MARGIN + first - (stride * (KL - levels) if dk > 0 else 0) + (0 if dx else x)
            parts.append(got[dx, dk][pl.ds(at, KL, stride=stride) if stride > 1 else slice(at, at + KL), :])
        return jnp.concatenate(parts, axis=0)

    held_x = {n: [x for x in range(-3, 7) if 0 <= x < ROWS or (n, x + ROWS) in EASTWARD and x < 0 or (n, x - ROWS) in WESTWARD and x >= ROWS] for n in NAMES}
    field = {n: {x: column(n, x) for x in held_x[n]} for n in NAMES}
    p, u, v, w = field["p"], field["u"], field["v"], field["w"]
    for n in range(3):
        p, u, v, w = substep(n, p, u, v, w, *[field[m] for m in ("cx", "sl", "cy", "cz", "cp")])

    mid = slice(KL, 2 * KL)
    for x in range(ROWS):
        fields = jnp.concatenate([a[x][mid] for a in (p, u, v, w)], axis=0)
        cur[x] = fields
        feat_s[x] = fields.astype(BF16)

    def feature_copy(n):
        to = peers[n]
        return pltpu.make_async_remote_copy(
            src_ref=feat_s.at[to], dst_ref=feat_r.at[lev], send_sem=feat_ss.at[n], recv_sem=feat_rs.at[n],
            device_id=(tile, to), device_id_type=MESH,
        )

    for n in (1, 2, 0):
        feature_copy(n).start()
    fl[...] = jnp.zeros_like(fl)

    def take(features, s):
        for f in range(4):
            a = features[KL * f : KL * f + KL].astype(F32)
            at = pl.ds(pl.multiple_of(s * KL, KL), KL)
            fm[f, at] = a
            fl[at, f, :] = a
        key_chunk(s * KL, KL // 2, fl, lk, rk, rs, eq)

    take(feat_s[lev], lev)
    for n, s in enumerate(peers):
        feature_copy(n).wait_recv()
        take(feat_r[s], s)

    def tendency_copy(n):
        to = peers[n]
        return pltpu.make_async_remote_copy(
            src_ref=tend_s.at[to], dst_ref=tend_r.at[lev], send_sem=tend_ss.at[n], recv_sem=tend_rs.at[n],
            device_id=(tile, to), device_id_type=MESH,
        )

    turns = (1, 2, 0)
    blocks = [peers[n] for n in turns] + [lev]

    def done(n):
        d, j = n // (KL // 2), n % (KL // 2)
        if j == KL // 2 - 1:
            to = blocks[d]
            for f in range(4):
                tend_s[to, KL * f : KL * f + KL] = ot[pl.ds(pl.multiple_of(to * KL, KL), KL), f, :]
            if d < levs - 1:
                tendency_copy(turns[d]).start()

    query_pairs(
        [to * KL + k for to in blocks for k in range(0, KL, 2)], fl, fm, bias, ls, lf, tcol, rk, rs, eq, ot, done
    )
    tend_r[lev] = tend_s[lev]
    for n in range(levs - 1):
        feature_copy(n).wait_send()
        tendency_copy(n).wait()
    for x in range(ROWS):
        for f in range(4):
            rows = slice(KL * f, KL * f + KL)
            out[pl.ds(f * KL * ROWS + x, KL, stride=ROWS), :] = cur[x, rows] + tend_r[x, rows]


def shards(state, coef_x, coef_y, coef_z, slope, compress, ground, w_in, level_table, gain_attn,
           w_query, w_key, w_value, w_mix, temper, gain_head, w_tend):
    tiles, levs = lax.axis_size("tile"), lax.axis_size("lev")
    dma = pltpu.SemaphoreType.DMA

    def buf(*shape, dtype=F32):
        return pltpu.VMEM(shape, dtype)

    def pair(*shape):
        return [buf(*shape), buf(*shape)]

    flat = KL * ROWS
    operands = (
        state.reshape(4 * flat, CELLS), *[a.reshape(flat, CELLS) for a in (coef_x, coef_y, coef_z, slope, compress)],
        ground, temper.reshape(1, HEADS), w_in, level_table, gain_attn.reshape(1, WIDTH), gain_head.reshape(1, WIDTH),
        w_tend.T, w_query, w_key, w_value, w_mix,
    )
    result = pl.pallas_call(
        lambda *refs: whole(tiles, levs, *refs),
        out_shape=jax.ShapeDtypeStruct((4 * flat, CELLS), F32),
        in_specs=[pl.BlockSpec(memory_space=pl.ANY)] * len(operands),
        out_specs=pl.BlockSpec(memory_space=pltpu.VMEM),
        scratch_shapes=[
            *[buf(*a.shape, dtype=a.dtype) for a in operands], dma((len(operands),)),
            buf(LEVELS, 8, CELLS), buf(LEVELS, 8, CELLS),
            buf(48, 128, dtype=BF16), buf(368, 128, dtype=BF16), buf(528, 512, dtype=BF16),
            buf(8, 128), buf(HEADS, LEVELS, CELLS), buf(LEVELS, CELLS), buf(LEVELS, CELLS), buf(LEVELS, CELLS),
            buf(4, LEVELS, CELLS),
            dma((len(ROUTES),)), dma((len(ROUTES),)),
            *[buf(levs, 4 * KL, CELLS, dtype=BF16)] * 2, dma((levs - 1,)), dma((levs - 1,)),
            *pair(levs, 4 * KL, CELLS), dma((levs - 1,)), dma((levs - 1,)),
            buf(ROWS, 4 * KL, CELLS),
            *[buf(slots(*r)[1], CELLS, dtype=BF16) for r in ROUTES] * 2,
            *[buf(slots(*r)[1] + 2 * MARGIN, CELLS) for r in ROUTES],
        ],
        compiler_params=pltpu.CompilerParams(
            collective_id=0, has_side_effects=True, vmem_limit_bytes=60 * 2**20
        ),
        name="substeps_and_columns",
    )(*operands)
    return result.reshape(4, KL, ROWS, CELLS)


def solution(mesh):
    block = P("lev", "tile", None)
    placed = (P(None, "lev", "tile", None),) + (block,) * 5 + (P("tile", None),) + (P(),) * 10
    return jax.shard_map(
        shards, mesh=mesh, in_specs=placed, out_specs=P(None, "lev", "tile", None), check_vma=False
    )
```

```python
import math

import jax
import jax.numpy as jnp
from jax import lax
from jax.experimental import pallas as pl
from jax.experimental.pallas import tpu as pltpu
from jax.sharding import PartitionSpec as P

EPS = 1e-6
F32, BF16 = jnp.float32, jnp.bfloat16
LOG2E = math.log2(math.e)
HEADS, WIDTH, LEVELS, CELLS = 8, 512, 32, 128
HS = WIDTH // HEADS
X = 40


def dot(a, b):
    return jnp.dot(a, b, preferred_element_type=F32)


def dot_t(a, b):
    return lax.dot_general(a, b, (((1,), (1,)), ((), ())), precision=lax.Precision.HIGHEST, preferred_element_type=F32)


def split3(a):
    hi = a.astype(BF16).astype(F32)
    mid = (a - hi).astype(BF16).astype(F32)
    return hi, mid, a - hi - mid


def spread(a):
    hi, mid, lo = split3(a)
    return (hi + pltpu.roll(mid, X, 1) + pltpu.roll(lo, 2 * X, 1)).astype(BF16)


def prepare_maps(w_in, table, gain_attn, wq, wk, wv, wm, gain_head, w_tend, temper, lk, ls, lf, tcol):
    emb = jnp.concatenate([w_in[...].astype(F32), jnp.zeros((4, WIDTH), F32), table[...]], axis=0)
    xg3 = jnp.concatenate(split3(emb * gain_attn[...]), axis=0).astype(BF16)

    def through(w):
        a = dot(xg3, w[...])
        return a[:X] + a[X : 2 * X] + a[2 * X :]

    aq, ak, av = through(wq), through(wk), through(wv)
    pad = jnp.zeros((128 - X, WIDTH), F32)
    aq_p = jnp.concatenate([aq, pad], axis=0)
    ak_p = jnp.concatenate([ak, pad], axis=0)
    head = lax.broadcasted_iota(jnp.int32, (X, WIDTH), 1) // HS

    def by_head(a):
        return jnp.concatenate([jnp.where(head == h, a, 0.0) for h in range(HEADS)], axis=0)

    kb = by_head(ak)
    qb = by_head(aq)
    s_map = dot_t(kb, aq_p)
    kk = dot_t(kb, ak_p)
    qq = dot_t(qb, aq_p)
    ee = dot_t(emb, jnp.concatenate([emb, pad], axis=0))
    lane = lax.broadcasted_iota(jnp.int32, (1, 128), 1)
    twice = jnp.where(lane < 8, 1.0, 2.0)
    r40 = lax.broadcasted_iota(jnp.int32, (X, 128), 0)
    l40 = lax.broadcasted_iota(jnp.int32, (X, 128), 1)
    diag = (r40 == l40) & (r40 >= 8)

    def norm_rows(g):
        return [g[i : i + 1] * twice for i in range(4)] + [jnp.sum(jnp.where(diag, g, 0.0), axis=0, keepdims=True)]

    def norm_map(gram):
        per = [norm_rows(gram[X * h : X * h + X]) for h in range(HEADS)]
        return jnp.concatenate([per[h][i] for i in range(5) for h in range(HEADS)], axis=0)

    e_rows = norm_rows(ee) + [jnp.zeros((3, 128), F32)]
    lk[...] = spread(jnp.concatenate([norm_map(kk)] + e_rows, axis=0))
    ls[0:320] = spread(s_map)
    ls[320:360] = spread(norm_map(qq))
    ls[360:368] = jnp.zeros((8, 128), BF16)

    vh, vm, _ = split3(by_head(av))
    c = dot(vh.astype(BF16), wm[...]) + dot(vm.astype(BF16), wm[...])
    eh, em, el = split3(emb)
    rows = [c[X * h + 8 : X * h + X] for h in range(HEADS)]
    rows += [jnp.broadcast_to(c[X * h + i : X * h + i + 1], (4, WIDTH)) for h in range(HEADS) for i in range(4)]
    rows += [eh, em, el, jnp.zeros((8, WIDTH), F32)]
    lft = jnp.concatenate(rows, axis=0)
    wt = jnp.concatenate([w_tend[...].astype(F32), jnp.zeros((12, WIDTH), F32)], axis=0) * gain_head[...]
    t = dot_t(wt, lft)
    th = t[:8].astype(BF16).astype(F32)
    lf[0:512] = lft.T.astype(BF16)
    lf[512:528] = jnp.concatenate([th, t[:8] - th], axis=0).astype(BF16)
    square = (HEADS, HEADS)
    on_diag = lax.broadcasted_iota(jnp.int32, square, 0) == lax.broadcasted_iota(jnp.int32, square, 1)
    scale = jnp.sum(jnp.where(on_diag, temper[...], 0.0), axis=1, keepdims=True) * (LOG2E / math.sqrt(HS))
    tcol[...] = jnp.broadcast_to(scale, (HEADS, 128))


def token_rows(fl, l):
    lev = lax.broadcasted_iota(jnp.int32, (LEVELS, CELLS), 0) == l
    one = jnp.concatenate([fl[l], lev.astype(F32)], axis=0)
    return jnp.concatenate([one, one, one, jnp.zeros((8, CELLS), F32)], axis=0).astype(BF16)


def norms_at(out, f, base, epsq, scale):
    n = out[base + 32 : base + 40]
    for i in range(4):
        n = n + f[i : i + 1] * out[base + 8 * i : base + 8 * i + 8]
    return lax.rsqrt(jnp.maximum(n, 0.0) * (1.0 / HS) + epsq) * scale


def key_chunk(base, pairs, fl, lk, rk, rs, eq):
    for l0 in [base + 2 * j for j in range(pairs)]:
        x = jnp.concatenate([token_rows(fl, l0), token_rows(fl, l0 + 1)], axis=1)
        both = dot(lk[...], x)
        for a in range(2):
            l = l0 + a
            out = both[:, 128 * a : 128 * a + 128]
            f = fl[l]
            n = out[44:45]
            for i in range(4):
                n = n + f[i : i + 1] * out[40 + i : 41 + i]
            ms = jnp.maximum(n, 0.0) * (1.0 / WIDTH) + EPS
            rs[pl.ds(l, 1), :] = lax.rsqrt(ms)
            eq[pl.ds(l, 1), :] = EPS * ms
            rk[:, l, :] = norms_at(out, f, 0, EPS * ms, 1.0)


def score_terms(l0, fl, ls):
    x = jnp.concatenate([token_rows(fl, l0), token_rows(fl, l0 + 1)], axis=1)
    return x, dot(ls[...], x)


def attend(l0, x, out, fl, fm, bias, tcol, rk, rs, eq):
    parts = []
    low = lax.broadcasted_iota(jnp.int32, (8, CELLS), 0) < 4
    for a in range(2):
        o = out[:, 128 * a : 128 * a + 128]
        rq = norms_at(o, fl[l0 + a], 320, eq[pl.ds(l0 + a, 1), :], tcol[...])
        probs, sums = [], []
        for h in range(HEADS):
            s = o[X * h + 8 : X * h + X]
            for i in range(4):
                s = s + fm[i] * o[X * h + i : X * h + i + 1]
            s = s * rk[h] * rq[h : h + 1] + bias[...]
            p = jnp.exp2(s - jnp.max(s, axis=0, keepdims=True))
            p = p * (1.0 / jnp.sum(p, axis=0, keepdims=True)) * rs[...]
            probs.append(p)
            pb = p.astype(BF16)
            z = [pb * fm[i].astype(BF16) for i in range(4)]
            z = [(a[0:16] + a[16:32]).astype(F32) for a in z]
            z = [a[0:8] + a[8:16] for a in z]
            for i in (0, 2):
                sums.append(jnp.where(low, z[i], z[i + 1]) + pltpu.roll(jnp.where(low, z[i + 1], z[i]), 4, 0))
        parts.append(jnp.concatenate(probs + sums, axis=0).astype(BF16))
    return jnp.concatenate([jnp.concatenate(parts, axis=1), x], axis=0)


def finish(l0, rhs, lf, ot):
    fin = dot(lf[...], rhs)
    stream = fin[:512]
    ms = jnp.mean(stream * stream, axis=0, keepdims=True)
    tend = (fin[512:520] + fin[520:528]) * lax.rsqrt(ms + EPS)
    ot[l0] = tend[:, :128]
    ot[l0 + 1] = tend[:, 128:]


def query_pairs(levels, fl, fm, bias, ls, lf, tcol, rk, rs, eq, ot, done=lambda n: None, early=()):
    pairs = len(levels)
    first, second = {}, {}
    for step in range(pairs + 2):
        if step < pairs:
            first[step] = early[step] if step in early else score_terms(levels[step], fl, ls)
        if step >= 2:
            finish(levels[step - 2], second.pop(step - 2), lf, ot)
            done(step - 2)
        if 1 <= step <= pairs:
            second[step - 1] = attend(levels[step - 1], *first.pop(step - 1), fl, fm, bias, tcol, rk, rs, eq)


ROWS = 4
KL = 8
MESH = pl.DeviceIdType.MESH


NAMES = ("p", "u", "v", "w", "cx", "cy", "cz", "sl", "cp")
EASTWARD = [(n, x) for n in NAMES for x in range(1 if n in ("p", "u", "cx", "sl") else 2, ROWS)]
WESTWARD = [(n, x) for n in NAMES for x in range(3 if n == "p" else 2)]
ROUTES = [(dx, dk) for dx in (1, -1, 0) for dk in (0, 1, -1) if (dx, dk) != (0, 0)]
MARGIN = 32


def slots(dx, dk):
    tall = ("p", "w", "cz")
    if dx == 0:
        wanted = [((n, None), 3 if n in tall else 2) for n in NAMES]
    elif dk == 0:
        wanted = [(s, KL) for s in (EASTWARD if dx > 0 else WESTWARD)]
    elif dx > 0:
        wanted = [(s, 3 if s[0] == "p" or s[0] in tall and dk > 0 else 2) for s in EASTWARD]
    else:
        wanted = [((n, x), 2 - x if n in tall else 1) for n in NAMES for x in range(2 if n in tall else 1)]
    table, row = {}, 0
    for key, levels in wanted:
        table[key] = row, levels
        row += levels * (ROWS if dx == 0 else 1)
    return table, -(-row // 16) * 16


def substep(n, p, u, v, w, cx, sl, cy, cz, cp):
    up = {x: pltpu.roll(a, 3 * KL - 1, 0) for x, a in p.items()}
    down = {x: pltpu.roll(a, 1, 0) for x, a in p.items()}
    u = {
        x: u[x] - cx[x] * (p[x + 1] - p[x]) - 0.5 * sl[x] * (up[x] - down[x])
        for x in range(n - 3, ROWS + 2 - n)
    }
    new_p, new_v, new_w = {}, {}, {}
    for x in range(n - 2, ROWS + 2 - n):
        c = p[x]
        wx = w[x] - cz[x] * (up[x] - c)
        vx = v[x] - cy[x] * (pltpu.roll(c, CELLS - 1, 1) - c)
        div = (u[x] - u[x - 1]) + (vx - pltpu.roll(vx, 1, 1)) + (wx - pltpu.roll(wx, 1, 0))
        new_p[x] = c - cp[x] * div
        new_v[x] = vx
        new_w[x] = wx
    return new_p, u, new_v, new_w


def whole(tiles, levs, *refs):
    hbm, out, held, in_sem, rest = refs[:17], refs[17], refs[18:35], refs[35], refs[36:]
    (state, coef_x, coef_y, coef_z, slope, compress, ground, temper, w_in, table, gain_attn, gain_head, w_tend,
     wq, wk, wv, wm) = held
    (fl, ot, lk, ls, lf, tcol, rk, rs, eq, bias, fm,
     halo_ss, halo_rs, feat_s, feat_r, feat_ss, feat_rs, tend_s, tend_r, tend_ss, tend_rs, cur) = rest[:22]
    halo_s, halo_r, wide = rest[22:30], rest[30:38], rest[38:46]
    tile, lev = lax.axis_index("tile"), lax.axis_index("lev")
    near = lev + 1 - 2 * lax.rem(lev, 2)
    peers = [near, lax.rem(lev + 2, levs), lax.rem(near + 2, levs)]
    there = [
        (tile + dx >= 0) & (tile + dx < tiles) & (lev + dk >= 0) & (lev + dk < levs) for dx, dk in ROUTES
    ]
    source_there = [there[ROUTES.index((-dx, -dk))] for dx, dk in ROUTES]

    barrier = pltpu.get_barrier_semaphore()
    for (dx, dk), exists in zip(ROUTES, there):
        if dx:
            @pl.when(exists)
            def _():
                pl.semaphore_signal(barrier, inc=1, device_id=(tile + dx, lev + dk), device_id_type=MESH)
    for to in peers:
        pl.semaphore_signal(barrier, inc=1, device_id=(tile, to), device_id_type=MESH)

    loads = [pltpu.make_async_copy(src, dst, in_sem.at[n]) for n, (src, dst) in enumerate(zip(hbm, held))]
    for copy in loads:
        copy.start()
    for copy in loads[:6]:
        copy.wait()
    held_by = dict(zip(NAMES, [(state, f) for f in range(4)] + [(a, 0) for a in (coef_x, coef_y, coef_z, slope, compress)]))

    def slab(name, x, k=0, count=KL):
        ref, f = held_by[name]
        return ref[pl.ds((f * KL + k) * ROWS + x, count, stride=ROWS), :]

    for i, (dx, dk) in enumerate(ROUTES):
        layout, rows = slots(dx, dk)
        pieces = []
        for (name, x), (_, levels) in layout.items():
            k = KL - levels if dk > 0 else 0
            if dx == 0:
                ref, f = held_by[name]
                pieces.append(ref[(f * KL + k) * ROWS : (f * KL + k + levels) * ROWS, :])
            else:
                pieces.append(slab(name, x, k, levels))
        extra = rows - sum(a.shape[0] for a in pieces)
        if extra:
            pieces.append(jnp.zeros((extra, CELLS), F32))
        halo_s[i][...] = jnp.concatenate(pieces, axis=0).astype(BF16)

        @pl.when(jnp.logical_not(source_there[i]))
        def _():
            halo_r[i][...] = jnp.zeros_like(halo_r[i])

    def halo_copy(i):
        dx, dk = ROUTES[i]
        return pltpu.make_async_remote_copy(
            src_ref=halo_s[i], dst_ref=halo_r[i], send_sem=halo_ss.at[i], recv_sem=halo_rs.at[i],
            device_id=(tile + dx, lev + dk), device_id_type=MESH,
        )

    beside = [exists.astype(jnp.int32) for (dx, dk), exists in zip(ROUTES, there) if dx]
    pl.semaphore_wait(barrier, levs - 1 + sum(beside))
    for i in (1, 2, 0, 4, 5, 3, 6, 7):
        @pl.when(there[i])
        def _():
            halo_copy(i).start()

    for copy in loads[6:]:
        copy.wait()
    m_level = lax.broadcasted_iota(jnp.int32, (LEVELS, CELLS), 0)
    bias[...] = jnp.where(m_level >= ground[pl.ds(lev, 1), :], 0.0, -1e30)
    prepare_maps(w_in, table, gain_attn, wq, wk, wv, wm, gain_head, w_tend, temper, lk, ls, lf, tcol)

    for i in range(len(ROUTES)):
        @pl.when(there[i])
        def _():
            halo_copy(i).wait_send()

        @pl.when(source_there[i])
        def _():
            halo_copy(i).wait_recv()

    got = {}
    for i, (dx, dk) in enumerate(ROUTES):
        rows = slots(dx, dk)[1]
        wide[i][0:MARGIN] = jnp.zeros((MARGIN, CELLS), F32)
        wide[i][MARGIN : MARGIN + rows] = halo_r[i][...].astype(F32)
        wide[i][MARGIN + rows :] = jnp.zeros((MARGIN, CELLS), F32)
        got[dx, dk] = wide[i]

    def column(name, x):
        dx = 1 if x < 0 else -1 if x >= ROWS else 0
        key = (name, x + ROWS * dx if dx else None)
        parts = []
        for dk in (1, 0, -1):
            if dx == 0 and dk == 0:
                parts.append(slab(name, x))
                continue
            first, levels = slots(dx, dk)[0].get(key, (None, 0))
            if levels == 0:
                parts.append(jnp.zeros((KL, CELLS), F32))
                continue
            stride = 1 if dx else ROWS
            at = MARGIN + first - (stride * (KL - levels) if dk > 0 else 0) + (0 if dx else x)
            parts.append(got[dx, dk][pl.ds(at, KL, stride=stride) if stride > 1 else slice(at, at + KL), :])
        return jnp.concatenate(parts, axis=0)

    held_x = {n: [x for x in range(-3, 7) if 0 <= x < ROWS or (n, x + ROWS) in EASTWARD and x < 0 or (n, x - ROWS) in WESTWARD and x >= ROWS] for n in NAMES}
    field = {n: {x: column(n, x) for x in held_x[n]} for n in NAMES}
    p, u, v, w = field["p"], field["u"], field["v"], field["w"]
    for n in range(3):
        p, u, v, w = substep(n, p, u, v, w, *[field[m] for m in ("cx", "sl", "cy", "cz", "cp")])

    mid = slice(KL, 2 * KL)
    for x in range(ROWS):
        fields = jnp.concatenate([a[x][mid] for a in (p, u, v, w)], axis=0)
        cur[x] = fields
        feat_s[x] = fields.astype(BF16)

    def feature_copy(n):
        to = peers[n]
        return pltpu.make_async_remote_copy(
            src_ref=feat_s.at[to], dst_ref=feat_r.at[lev], send_sem=feat_ss.at[n], recv_sem=feat_rs.at[n],
            device_id=(tile, to), device_id_type=MESH,
        )

    for n in (1, 2, 0):
        feature_copy(n).start()
    fl[...] = jnp.zeros_like(fl)

    def take(features, s):
        for f in range(4):
            a = features[KL * f : KL * f + KL].astype(F32)
            at = pl.ds(pl.multiple_of(s * KL, KL), KL)
            fm[f, at] = a
            fl[at, f, :] = a
        key_chunk(s * KL, KL // 2, fl, lk, rk, rs, eq)

    take(feat_s[lev], lev)
    early = {12 + j: score_terms(lev * KL + 2 * j, fl, ls) for j in range(KL // 2)}
    for n, s in enumerate(peers):
        feature_copy(n).wait_recv()
        take(feat_r[s], s)

    def tendency_copy(n):
        to = peers[n]
        return pltpu.make_async_remote_copy(
            src_ref=tend_s.at[to], dst_ref=tend_r.at[lev], send_sem=tend_ss.at[n], recv_sem=tend_rs.at[n],
            device_id=(tile, to), device_id_type=MESH,
        )

    turns = (1, 2, 0)
    blocks = [peers[n] for n in turns] + [lev]

    def done(n):
        d, j = n // (KL // 2), n % (KL // 2)
        if j == KL // 2 - 1:
            to = blocks[d]
            for f in range(4):
                tend_s[to, KL * f : KL * f + KL] = ot[pl.ds(pl.multiple_of(to * KL, KL), KL), f, :]
            if d < levs - 1:
                tendency_copy(turns[d]).start()

    query_pairs(
        [to * KL + k for to in blocks for k in range(0, KL, 2)], fl, fm, bias, ls, lf, tcol, rk, rs, eq, ot, done, early
    )
    tend_r[lev] = tend_s[lev]
    for n in range(levs - 1):
        feature_copy(n).wait_send()
        tendency_copy(n).wait()
    for x in range(ROWS):
        for f in range(4):
            rows = slice(KL * f, KL * f + KL)
            out[pl.ds(f * KL * ROWS + x, KL, stride=ROWS), :] = cur[x, rows] + tend_r[x, rows]


def shards(state, coef_x, coef_y, coef_z, slope, compress, ground, w_in, level_table, gain_attn,
           w_query, w_key, w_value, w_mix, temper, gain_head, w_tend):
    tiles, levs = lax.axis_size("tile"), lax.axis_size("lev")
    dma = pltpu.SemaphoreType.DMA

    def buf(*shape, dtype=F32):
        return pltpu.VMEM(shape, dtype)

    def pair(*shape):
        return [buf(*shape), buf(*shape)]

    flat = KL * ROWS
    operands = (
        state.reshape(4 * flat, CELLS), *[a.reshape(flat, CELLS) for a in (coef_x, coef_y, coef_z, slope, compress)],
        ground, temper.reshape(1, HEADS), w_in, level_table, gain_attn.reshape(1, WIDTH), gain_head.reshape(1, WIDTH),
        w_tend.T, w_query, w_key, w_value, w_mix,
    )
    result = pl.pallas_call(
        lambda *refs: whole(tiles, levs, *refs),
        out_shape=jax.ShapeDtypeStruct((4 * flat, CELLS), F32),
        in_specs=[pl.BlockSpec(memory_space=pl.ANY)] * len(operands),
        out_specs=pl.BlockSpec(memory_space=pltpu.VMEM),
        scratch_shapes=[
            *[buf(*a.shape, dtype=a.dtype) for a in operands], dma((len(operands),)),
            buf(LEVELS, 8, CELLS), buf(LEVELS, 8, CELLS),
            buf(48, 128, dtype=BF16), buf(368, 128, dtype=BF16), buf(528, 512, dtype=BF16),
            buf(8, 128), buf(HEADS, LEVELS, CELLS), buf(LEVELS, CELLS), buf(LEVELS, CELLS), buf(LEVELS, CELLS),
            buf(4, LEVELS, CELLS),
            dma((len(ROUTES),)), dma((len(ROUTES),)),
            *[buf(levs, 4 * KL, CELLS, dtype=BF16)] * 2, dma((levs - 1,)), dma((levs - 1,)),
            *pair(levs, 4 * KL, CELLS), dma((levs - 1,)), dma((levs - 1,)),
            buf(ROWS, 4 * KL, CELLS),
            *[buf(slots(*r)[1], CELLS, dtype=BF16) for r in ROUTES] * 2,
            *[buf(slots(*r)[1] + 2 * MARGIN, CELLS) for r in ROUTES],
        ],
        compiler_params=pltpu.CompilerParams(
            collective_id=0, has_side_effects=True, vmem_limit_bytes=60 * 2**20
        ),
        name="substeps_and_columns",
    )(*operands)
    return result.reshape(4, KL, ROWS, CELLS)


def solution(mesh):
    block = P("lev", "tile", None)
    placed = (P(None, "lev", "tile", None),) + (block,) * 5 + (P("tile", None),) + (P(),) * 10
    return jax.shard_map(
        shards, mesh=mesh, in_specs=placed, out_specs=P(None, "lev", "tile", None), check_vma=False
    )
```

```python
import math

import jax
import jax.numpy as jnp
from jax import lax
from jax.experimental import pallas as pl
from jax.experimental.pallas import tpu as pltpu
from jax.sharding import PartitionSpec as P

EPS = 1e-6
F32, BF16 = jnp.float32, jnp.bfloat16
LOG2E = math.log2(math.e)
HEADS, WIDTH, LEVELS, CELLS = 8, 512, 32, 128
HS = WIDTH // HEADS
X = 40


def dot(a, b):
    return jnp.dot(a, b, preferred_element_type=F32)


def dot_t(a, b):
    return lax.dot_general(a, b, (((1,), (1,)), ((), ())), precision=lax.Precision.HIGHEST, preferred_element_type=F32)


def split3(a):
    hi = a.astype(BF16).astype(F32)
    mid = (a - hi).astype(BF16).astype(F32)
    return hi, mid, a - hi - mid


def spread(a):
    hi, mid, lo = split3(a)
    return (hi + pltpu.roll(mid, X, 1) + pltpu.roll(lo, 2 * X, 1)).astype(BF16)


def prepare_maps(w_in, table, gain_attn, wq, wk, wv, wm, gain_head, w_tend, temper, lk, ls, lf, tcol):
    emb = jnp.concatenate([w_in[...].astype(F32), jnp.zeros((4, WIDTH), F32), table[...]], axis=0)
    xg3 = jnp.concatenate(split3(emb * gain_attn[...]), axis=0).astype(BF16)

    def through(w):
        a = dot(xg3, w[...])
        return a[:X] + a[X : 2 * X] + a[2 * X :]

    aq, ak, av = through(wq), through(wk), through(wv)
    pad = jnp.zeros((128 - X, WIDTH), F32)
    aq_p = jnp.concatenate([aq, pad], axis=0)
    ak_p = jnp.concatenate([ak, pad], axis=0)
    head = lax.broadcasted_iota(jnp.int32, (X, WIDTH), 1) // HS

    def by_head(a):
        return jnp.concatenate([jnp.where(head == h, a, 0.0) for h in range(HEADS)], axis=0)

    kb = by_head(ak)
    qb = by_head(aq)
    s_map = dot_t(kb, aq_p)
    kk = dot_t(kb, ak_p)
    qq = dot_t(qb, aq_p)
    ee = dot_t(emb, jnp.concatenate([emb, pad], axis=0))
    lane = lax.broadcasted_iota(jnp.int32, (1, 128), 1)
    twice = jnp.where(lane < 8, 1.0, 2.0)
    r40 = lax.broadcasted_iota(jnp.int32, (X, 128), 0)
    l40 = lax.broadcasted_iota(jnp.int32, (X, 128), 1)
    diag = (r40 == l40) & (r40 >= 8)

    def norm_rows(g):
        return [g[i : i + 1] * twice for i in range(4)] + [jnp.sum(jnp.where(diag, g, 0.0), axis=0, keepdims=True)]

    def norm_map(gram):
        per = [norm_rows(gram[X * h : X * h + X]) for h in range(HEADS)]
        return jnp.concatenate([per[h][i] for i in range(5) for h in range(HEADS)], axis=0)

    e_rows = norm_rows(ee) + [jnp.zeros((3, 128), F32)]
    lk[...] = spread(jnp.concatenate([norm_map(kk)] + e_rows, axis=0))
    ls[0:320] = spread(s_map)
    ls[320:360] = spread(norm_map(qq))
    ls[360:368] = jnp.zeros((8, 128), BF16)

    vh, vm, _ = split3(by_head(av))
    c = dot(vh.astype(BF16), wm[...]) + dot(vm.astype(BF16), wm[...])
    eh, em, el = split3(emb)
    rows = [c[X * h + 8 : X * h + X] for h in range(HEADS)]
    rows += [jnp.broadcast_to(c[X * h + i : X * h + i + 1], (4, WIDTH)) for h in range(HEADS) for i in range(4)]
    rows += [eh, em, el, jnp.zeros((8, WIDTH), F32)]
    lft = jnp.concatenate(rows, axis=0)
    wt = jnp.concatenate([w_tend[...].astype(F32), jnp.zeros((12, WIDTH), F32)], axis=0) * gain_head[...]
    t = dot_t(wt, lft)
    th = t[:8].astype(BF16).astype(F32)
    lf[0:512] = lft.T.astype(BF16)
    lf[512:528] = jnp.concatenate([th, t[:8] - th], axis=0).astype(BF16)
    square = (HEADS, HEADS)
    on_diag = lax.broadcasted_iota(jnp.int32, square, 0) == lax.broadcasted_iota(jnp.int32, square, 1)
    scale = jnp.sum(jnp.where(on_diag, temper[...], 0.0), axis=1, keepdims=True) * (LOG2E / math.sqrt(HS))
    tcol[...] = jnp.broadcast_to(scale, (HEADS, 128))


def token_rows(fl, l):
    lev = lax.broadcasted_iota(jnp.int32, (LEVELS, CELLS), 0) == l
    one = jnp.concatenate([fl[l], lev.astype(F32)], axis=0)
    return jnp.concatenate([one, one, one, jnp.zeros((8, CELLS), F32)], axis=0).astype(BF16)


def norms_at(out, f, base, epsq, scale):
    n = out[base + 32 : base + 40]
    for i in range(4):
        n = n + f[i : i + 1] * out[base + 8 * i : base + 8 * i + 8]
    return lax.rsqrt(jnp.maximum(n, 0.0) * (1.0 / HS) + epsq) * scale


def key_chunk(base, pairs, fl, lk, rk, rs, eq):
    for l0 in [base + 2 * j for j in range(pairs)]:
        x = jnp.concatenate([token_rows(fl, l0), token_rows(fl, l0 + 1)], axis=1)
        both = dot(lk[...], x)
        for a in range(2):
            l = l0 + a
            out = both[:, 128 * a : 128 * a + 128]
            f = fl[l]
            n = out[44:45]
            for i in range(4):
                n = n + f[i : i + 1] * out[40 + i : 41 + i]
            ms = jnp.maximum(n, 0.0) * (1.0 / WIDTH) + EPS
            rs[pl.ds(l, 1), :] = lax.rsqrt(ms)
            eq[pl.ds(l, 1), :] = EPS * ms
            rk[:, l, :] = norms_at(out, f, 0, EPS * ms, 1.0)


def score_terms(l0, fl, ls):
    x = jnp.concatenate([token_rows(fl, l0), token_rows(fl, l0 + 1)], axis=1)
    return x, dot(ls[...], x)


def attend(l0, x, out, fl, fm, bias, tcol, rk, rs, eq):
    parts = []
    fb = [fm[i].astype(BF16) for i in range(4)]
    low = lax.broadcasted_iota(jnp.int32, (8, CELLS), 0) < 4
    for a in range(2):
        o = out[:, 128 * a : 128 * a + 128]
        rq = norms_at(o, fl[l0 + a], 320, eq[pl.ds(l0 + a, 1), :], tcol[...])
        probs, sums = [], []
        for h in range(HEADS):
            s = o[X * h + 8 : X * h + X]
            for i in range(4):
                s = s + fm[i] * o[X * h + i : X * h + i + 1]
            s = s * rk[h] * rq[h : h + 1] + bias[...]
            p = jnp.exp2(s - jnp.max(s, axis=0, keepdims=True))
            p = p * (1.0 / jnp.sum(p, axis=0, keepdims=True)) * rs[...]
            probs.append(p)
            pb = p.astype(BF16)
            z = [pb * b for b in fb]
            z = [(a[0:16] + a[16:32]).astype(F32) for a in z]
            z = [a[0:8] + a[8:16] for a in z]
            for i in (0, 2):
                sums.append(jnp.where(low, z[i], z[i + 1]) + pltpu.roll(jnp.where(low, z[i + 1], z[i]), 4, 0))
        parts.append(jnp.concatenate(probs + sums, axis=0).astype(BF16))
    return jnp.concatenate([jnp.concatenate(parts, axis=1), x], axis=0)


def finish(l0, rhs, lf, ot):
    fin = dot(lf[...], rhs)
    stream = fin[:512]
    ms = jnp.mean(stream * stream, axis=0, keepdims=True)
    tend = (fin[512:520] + fin[520:528]) * lax.rsqrt(ms + EPS)
    ot[l0] = tend[:, :128]
    ot[l0 + 1] = tend[:, 128:]


def query_pairs(levels, fl, fm, bias, ls, lf, tcol, rk, rs, eq, ot, done=lambda n: None, early=()):
    pairs = len(levels)
    first, second = {}, {}
    for step in range(pairs + 2):
        if step < pairs:
            first[step] = early[step] if step in early else score_terms(levels[step], fl, ls)
        if step >= 2:
            finish(levels[step - 2], second.pop(step - 2), lf, ot)
            done(step - 2)
        if 1 <= step <= pairs:
            second[step - 1] = attend(levels[step - 1], *first.pop(step - 1), fl, fm, bias, tcol, rk, rs, eq)


ROWS = 4
KL = 8
MESH = pl.DeviceIdType.MESH


NAMES = ("p", "u", "v", "w", "cx", "cy", "cz", "sl", "cp")
EASTWARD = [(n, x) for n in NAMES for x in range(1 if n in ("p", "u", "cx", "sl") else 2, ROWS)]
WESTWARD = [(n, x) for n in NAMES for x in range(3 if n == "p" else 2)]
ROUTES = [(dx, dk) for dx in (1, -1, 0) for dk in (0, 1, -1) if (dx, dk) != (0, 0)]
MARGIN = 32


def slots(dx, dk):
    tall = ("p", "w", "cz")
    if dx == 0:
        wanted = [((n, None), 3 if n in tall else 2) for n in NAMES]
    elif dk == 0:
        wanted = [(s, KL) for s in (EASTWARD if dx > 0 else WESTWARD)]
    elif dx > 0:
        wanted = [(s, 3 if s[0] == "p" or s[0] in tall and dk > 0 else 2) for s in EASTWARD]
    else:
        wanted = [((n, x), 2 - x if n in tall else 1) for n in NAMES for x in range(2 if n in tall else 1)]
    table, row = {}, 0
    for key, levels in wanted:
        table[key] = row, levels
        row += levels * (ROWS if dx == 0 else 1)
    return table, -(-row // 16) * 16


def substep(n, p, u, v, w, cx, sl, cy, cz, cp):
    up = {x: pltpu.roll(a, 3 * KL - 1, 0) for x, a in p.items()}
    down = {x: pltpu.roll(a, 1, 0) for x, a in p.items()}
    u = {
        x: u[x] - cx[x] * (p[x + 1] - p[x]) - 0.5 * sl[x] * (up[x] - down[x])
        for x in range(n - 3, ROWS + 2 - n)
    }
    new_p, new_v, new_w = {}, {}, {}
    for x in range(n - 2, ROWS + 2 - n):
        c = p[x]
        wx = w[x] - cz[x] * (up[x] - c)
        vx = v[x] - cy[x] * (pltpu.roll(c, CELLS - 1, 1) - c)
        div = (u[x] - u[x - 1]) + (vx - pltpu.roll(vx, 1, 1)) + (wx - pltpu.roll(wx, 1, 0))
        new_p[x] = c - cp[x] * div
        new_v[x] = vx
        new_w[x] = wx
    return new_p, u, new_v, new_w


def whole(tiles, levs, *refs):
    hbm, out, held, in_sem, rest = refs[:17], refs[17], refs[18:35], refs[35], refs[36:]
    (state, coef_x, coef_y, coef_z, slope, compress, ground, temper, w_in, table, gain_attn, gain_head, w_tend,
     wq, wk, wv, wm) = held
    (fl, ot, lk, ls, lf, tcol, rk, rs, eq, bias, fm,
     halo_ss, halo_rs, feat_s, feat_r, feat_ss, feat_rs, tend_s, tend_r, tend_ss, tend_rs, cur) = rest[:22]
    halo_s, halo_r, wide = rest[22:30], rest[30:38], rest[38:46]
    tile, lev = lax.axis_index("tile"), lax.axis_index("lev")
    near = lev + 1 - 2 * lax.rem(lev, 2)
    peers = [near, lax.rem(lev + 2, levs), lax.rem(near + 2, levs)]
    there = [
        (tile + dx >= 0) & (tile + dx < tiles) & (lev + dk >= 0) & (lev + dk < levs) for dx, dk in ROUTES
    ]
    source_there = [there[ROUTES.index((-dx, -dk))] for dx, dk in ROUTES]

    barrier = pltpu.get_barrier_semaphore()
    for (dx, dk), exists in zip(ROUTES, there):
        if dx:
            @pl.when(exists)
            def _():
                pl.semaphore_signal(barrier, inc=1, device_id=(tile + dx, lev + dk), device_id_type=MESH)
    for to in peers:
        pl.semaphore_signal(barrier, inc=1, device_id=(tile, to), device_id_type=MESH)

    loads = [pltpu.make_async_copy(src, dst, in_sem.at[n]) for n, (src, dst) in enumerate(zip(hbm, held))]
    for copy in loads:
        copy.start()
    for copy in loads[:6]:
        copy.wait()
    held_by = dict(zip(NAMES, [(state, f) for f in range(4)] + [(a, 0) for a in (coef_x, coef_y, coef_z, slope, compress)]))

    def slab(name, x, k=0, count=KL):
        ref, f = held_by[name]
        return ref[pl.ds((f * KL + k) * ROWS + x, count, stride=ROWS), :]

    for i, (dx, dk) in enumerate(ROUTES):
        layout, rows = slots(dx, dk)
        pieces = []
        for (name, x), (_, levels) in layout.items():
            k = KL - levels if dk > 0 else 0
            if dx == 0:
                ref, f = held_by[name]
                pieces.append(ref[(f * KL + k) * ROWS : (f * KL + k + levels) * ROWS, :])
            else:
                pieces.append(slab(name, x, k, levels))
        extra = rows - sum(a.shape[0] for a in pieces)
        if extra:
            pieces.append(jnp.zeros((extra, CELLS), F32))
        halo_s[i][...] = jnp.concatenate(pieces, axis=0).astype(BF16)

        @pl.when(jnp.logical_not(source_there[i]))
        def _():
            halo_r[i][...] = jnp.zeros_like(halo_r[i])

    def halo_copy(i):
        dx, dk = ROUTES[i]
        return pltpu.make_async_remote_copy(
            src_ref=halo_s[i], dst_ref=halo_r[i], send_sem=halo_ss.at[i], recv_sem=halo_rs.at[i],
            device_id=(tile + dx, lev + dk), device_id_type=MESH,
        )

    beside = [exists.astype(jnp.int32) for (dx, dk), exists in zip(ROUTES, there) if dx]
    pl.semaphore_wait(barrier, levs - 1 + sum(beside))
    for i in (1, 2, 0, 4, 5, 3, 6, 7):
        @pl.when(there[i])
        def _():
            halo_copy(i).start()

    for copy in loads[6:]:
        copy.wait()
    m_level = lax.broadcasted_iota(jnp.int32, (LEVELS, CELLS), 0)
    bias[...] = jnp.where(m_level >= ground[pl.ds(lev, 1), :], 0.0, -1e30)
    prepare_maps(w_in, table, gain_attn, wq, wk, wv, wm, gain_head, w_tend, temper, lk, ls, lf, tcol)

    for i in range(len(ROUTES)):
        @pl.when(there[i])
        def _():
            halo_copy(i).wait_send()

        @pl.when(source_there[i])
        def _():
            halo_copy(i).wait_recv()

    got = {}
    for i, (dx, dk) in enumerate(ROUTES):
        rows = slots(dx, dk)[1]
        wide[i][0:MARGIN] = jnp.zeros((MARGIN, CELLS), F32)
        wide[i][MARGIN : MARGIN + rows] = halo_r[i][...].astype(F32)
        wide[i][MARGIN + rows :] = jnp.zeros((MARGIN, CELLS), F32)
        got[dx, dk] = wide[i]

    def column(name, x):
        dx = 1 if x < 0 else -1 if x >= ROWS else 0
        key = (name, x + ROWS * dx if dx else None)
        parts = []
        for dk in (1, 0, -1):
            if dx == 0 and dk == 0:
                parts.append(slab(name, x))
                continue
            first, levels = slots(dx, dk)[0].get(key, (None, 0))
            if levels == 0:
                parts.append(jnp.zeros((KL, CELLS), F32))
                continue
            stride = 1 if dx else ROWS
            at = MARGIN + first - (stride * (KL - levels) if dk > 0 else 0) + (0 if dx else x)
            parts.append(got[dx, dk][pl.ds(at, KL, stride=stride) if stride > 1 else slice(at, at + KL), :])
        return jnp.concatenate(parts, axis=0)

    held_x = {n: [x for x in range(-3, 7) if 0 <= x < ROWS or (n, x + ROWS) in EASTWARD and x < 0 or (n, x - ROWS) in WESTWARD and x >= ROWS] for n in NAMES}
    field = {n: {x: column(n, x) for x in held_x[n]} for n in NAMES}
    p, u, v, w = field["p"], field["u"], field["v"], field["w"]
    for n in range(3):
        p, u, v, w = substep(n, p, u, v, w, *[field[m] for m in ("cx", "sl", "cy", "cz", "cp")])

    mid = slice(KL, 2 * KL)
    for x in range(ROWS):
        fields = jnp.concatenate([a[x][mid] for a in (p, u, v, w)], axis=0)
        cur[x] = fields
        feat_s[x] = fields.astype(BF16)

    def feature_copy(n):
        to = peers[n]
        return pltpu.make_async_remote_copy(
            src_ref=feat_s.at[to], dst_ref=feat_r.at[lev], send_sem=feat_ss.at[n], recv_sem=feat_rs.at[n],
            device_id=(tile, to), device_id_type=MESH,
        )

    for n in (1, 2, 0):
        feature_copy(n).start()
    fl[...] = jnp.zeros_like(fl)

    def take(features, s):
        for f in range(4):
            a = features[KL * f : KL * f + KL].astype(F32)
            at = pl.ds(pl.multiple_of(s * KL, KL), KL)
            fm[f, at] = a
            fl[at, f, :] = a
        key_chunk(s * KL, KL // 2, fl, lk, rk, rs, eq)

    take(feat_s[lev], lev)
    early = {12 + j: score_terms(lev * KL + 2 * j, fl, ls) for j in range(KL // 2)}
    for n, s in enumerate(peers):
        feature_copy(n).wait_recv()
        take(feat_r[s], s)

    def tendency_copy(n):
        to = peers[n]
        return pltpu.make_async_remote_copy(
            src_ref=tend_s.at[to], dst_ref=tend_r.at[lev], send_sem=tend_ss.at[n], recv_sem=tend_rs.at[n],
            device_id=(tile, to), device_id_type=MESH,
        )

    turns = (1, 2, 0)
    blocks = [peers[n] for n in turns] + [lev]

    def done(n):
        d, j = n // (KL // 2), n % (KL // 2)
        if j == KL // 2 - 1:
            to = blocks[d]
            for f in range(4):
                tend_s[to, KL * f : KL * f + KL] = ot[pl.ds(pl.multiple_of(to * KL, KL), KL), f, :]
            if d < levs - 1:
                tendency_copy(turns[d]).start()

    query_pairs(
        [to * KL + k for to in blocks for k in range(0, KL, 2)], fl, fm, bias, ls, lf, tcol, rk, rs, eq, ot, done, early
    )
    tend_r[lev] = tend_s[lev]
    for n in range(levs - 1):
        feature_copy(n).wait_send()
        tendency_copy(n).wait()
    for x in range(ROWS):
        for f in range(4):
            rows = slice(KL * f, KL * f + KL)
            out[pl.ds(f * KL * ROWS + x, KL, stride=ROWS), :] = cur[x, rows] + tend_r[x, rows]


def shards(state, coef_x, coef_y, coef_z, slope, compress, ground, w_in, level_table, gain_attn,
           w_query, w_key, w_value, w_mix, temper, gain_head, w_tend):
    tiles, levs = lax.axis_size("tile"), lax.axis_size("lev")
    dma = pltpu.SemaphoreType.DMA

    def buf(*shape, dtype=F32):
        return pltpu.VMEM(shape, dtype)

    def pair(*shape):
        return [buf(*shape), buf(*shape)]

    flat = KL * ROWS
    operands = (
        state.reshape(4 * flat, CELLS), *[a.reshape(flat, CELLS) for a in (coef_x, coef_y, coef_z, slope, compress)],
        ground, temper.reshape(1, HEADS), w_in, level_table, gain_attn.reshape(1, WIDTH), gain_head.reshape(1, WIDTH),
        w_tend.T, w_query, w_key, w_value, w_mix,
    )
    result = pl.pallas_call(
        lambda *refs: whole(tiles, levs, *refs),
        out_shape=jax.ShapeDtypeStruct((4 * flat, CELLS), F32),
        in_specs=[pl.BlockSpec(memory_space=pl.ANY)] * len(operands),
        out_specs=pl.BlockSpec(memory_space=pltpu.VMEM),
        scratch_shapes=[
            *[buf(*a.shape, dtype=a.dtype) for a in operands], dma((len(operands),)),
            buf(LEVELS, 8, CELLS), buf(LEVELS, 8, CELLS),
            buf(48, 128, dtype=BF16), buf(368, 128, dtype=BF16), buf(528, 512, dtype=BF16),
            buf(8, 128), buf(HEADS, LEVELS, CELLS), buf(LEVELS, CELLS), buf(LEVELS, CELLS), buf(LEVELS, CELLS),
            buf(4, LEVELS, CELLS),
            dma((len(ROUTES),)), dma((len(ROUTES),)),
            *[buf(levs, 4 * KL, CELLS, dtype=BF16)] * 2, dma((levs - 1,)), dma((levs - 1,)),
            *pair(levs, 4 * KL, CELLS), dma((levs - 1,)), dma((levs - 1,)),
            buf(ROWS, 4 * KL, CELLS),
            *[buf(slots(*r)[1], CELLS, dtype=BF16) for r in ROUTES] * 2,
            *[buf(slots(*r)[1] + 2 * MARGIN, CELLS) for r in ROUTES],
        ],
        compiler_params=pltpu.CompilerParams(
            collective_id=0, has_side_effects=True, vmem_limit_bytes=60 * 2**20
        ),
        name="substeps_and_columns",
    )(*operands)
    return result.reshape(4, KL, ROWS, CELLS)


def solution(mesh):
    block = P("lev", "tile", None)
    placed = (P(None, "lev", "tile", None),) + (block,) * 5 + (P("tile", None),) + (P(),) * 10
    return jax.shard_map(
        shards, mesh=mesh, in_specs=placed, out_specs=P(None, "lev", "tile", None), check_vma=False
    )
```
